512 devices in a mesh: ctx: 16 (over z), tp: 16 (over x, y), dp: 2 (over core).
Axes of the slice: x: 4, y: 4, z: 16, core: 2. Of those that a mesh axis runs over, the one named last changes fastest.
Arguments:
- queries: bfloat16 [4096, 4096], P(('dp', 'ctx'), 'tp'), parts along dimension 0, may hold values from -6 to 6
- keys: bfloat16 [4096, 4096], P(('dp', 'ctx'), 'tp'), parts along dimension 0, may hold values from -6 to 6
- values: bfloat16 [4096, 4096], P(('dp', 'ctx'), 'tp'), parts along dimension 0, may hold values from -6 to 6
- residues: float32 [4096, 16], P('tp'), may hold values from -1.5 to 1.5
- decays: float32 [4096, 16], P('tp'), as said below
- skip: float32 [4096], P('tp'), may hold values from -0.5 to 0.5
- out_weight: bfloat16 [4096, 4096], P('tp'), may hold values from -0.09375 to 0.09375
Outputs:
- projected: bfloat16 [4096, 4096], P(('dp', 'ctx', 'tp')), parts along dimension 0
The draws below stay inside these ranges and needn't reach their ends.
There are 2 independent parts, one for each index of `dp`. The reference program is written for one: setup_inputs(seed, part) draws one part's arguments, and reference() takes and returns one part's arrays. A program takes and returns all parts, laid end to end along the dimension named above; an argument that names none is the same for every part. Nothing has to cross between parts.
Inputs may be any that keep to these rules, and one draw needn't show every extreme that they name: `decays`: decay rates are at least 1 / 8192.
All inputs are finite; a program needn't handle non-finite values.
Results may differ from the reference program's by a relative error of at most 0.023.
Values may be sent and summed in bfloat16 or wider, within the bound.
A program may use at most 64 MiB of HBM per device.

```python
import jax
import jax.numpy as jnp
from jax import lax

D = 4096
S = 16
TOKENS = 2048
CH_DEV = 256
N_TP = 16


def draw_decays(key, part):
    key = jax.random.fold_in(key, 7)
    range_key = jax.random.fold_in(key, 0)
    lowest = 0.25 / TOKENS
    highest = 0.25
    uniform_draw = jax.random.uniform(range_key, (D, S), jnp.float32)
    return jnp.exp(jnp.log(lowest) + uniform_draw * (jnp.log(highest) - jnp.log(lowest)))


def block_levels(key, dims, cuts, least, largest):
    loudness = 1.0
    for axis_at, parts in cuts:
        steps = jax.random.uniform(jax.random.fold_in(jax.random.fold_in(key, 6), axis_at), (parts,), jnp.float32, least / len(cuts), largest / len(cuts))
        loudness = loudness * jnp.repeat(jnp.exp(steps), dims[axis_at] // parts).reshape((-1,) + (1,) * (len(dims) - 1 - axis_at))
    return loudness


def normal_values(rng, shape, width, bound, shards=(), held_as=jnp.bfloat16):
    loudness = block_levels(rng, shape, shards, -0.22, 0.18) if shards else 1.0
    array = jax.random.normal(rng, shape, jnp.float32) * width * loudness
    return jnp.minimum(jnp.maximum(array, -bound), bound).astype(held_as)


def setup_inputs(seed: int = 0, part: int = 0) -> dict:
    key_of = jax.random.split(jax.random.key(seed), 8)
    part_keys = jax.random.split(jax.random.fold_in(key_of[7], part), 8)
    queries = normal_values(part_keys[0], (TOKENS, D), 1.0, 6.0, ((0, 16), (1, 16)))
    keys = normal_values(part_keys[1], (TOKENS, D), 1.0, 6.0, ((0, 16), (1, 16)))
    values = normal_values(part_keys[2], (TOKENS, D), 1.0, 6.0, ((0, 16), (1, 16)))
    residues = normal_values(key_of[3], (D, S), S ** -0.5, 1.5, ((0, 16),), jnp.float32)
    decays = draw_decays(jax.random.fold_in(key_of[7], 71), part)
    skip = jnp.clip(jax.random.uniform(key_of[5], (D,), jnp.float32, -0.5, 0.5) * block_levels(key_of[5], (D,), ((0, 16),), -0.4, 0.0), -0.5, 0.5)
    out_weight = normal_values(key_of[6], (D, D), D ** -0.5, 0.09375, ((0, 16),))
    return {"queries": queries, "keys": keys, "values": values, "residues": residues, "decays": decays, "skip": skip, "out_weight": out_weight}


def modal_filter(residues, decays):
    positions = jnp.arange(TOKENS, dtype=jnp.float32)[:, None]
    kernel = jnp.zeros((TOKENS, D), jnp.float32)
    for mode_index in range(S):
        decay_rate = decays[:, mode_index]
        kernel = kernel + residues[:, mode_index] * jnp.sqrt(2.0 * decay_rate) * jnp.exp(-decay_rate * positions)
    return kernel

def reference(queries, keys, values, residues, decays, skip, out_weight):
    key_value = keys.astype(jnp.float32) * values.astype(jnp.float32)
    kernel = modal_filter(residues, decays)
    padded_len = 2 * TOKENS
    spectrum = jnp.fft.rfft(key_value, n=padded_len, axis=0) * jnp.fft.rfft(kernel, n=padded_len, axis=0)
    convolved = jnp.fft.irfft(spectrum, n=padded_len, axis=0)[:TOKENS]
    gated = (queries.astype(jnp.float32) * (convolved + skip[None, :] * key_value)).astype(jnp.bfloat16)
    groups = gated.reshape(TOKENS, N_TP, CH_DEV).transpose(1, 0, 2)
    blocks = out_weight.reshape(N_TP, CH_DEV, D)

    def add_group(running, group_pair):
        partial_value = jnp.dot(group_pair[0], group_pair[1], preferred_element_type=jnp.float32)
        rounded = lax.optimization_barrier(partial_value.astype(jnp.bfloat16))
        return (running + rounded.astype(jnp.float32), None)
    running, _ = lax.scan(add_group, jnp.zeros((TOKENS, D), jnp.float32), (groups, blocks))
    return running.astype(jnp.bfloat16)
```

```python
import functools

import jax
import jax.numpy as jnp
from jax import lax
from jax.experimental import pallas as pl
from jax.experimental.pallas import tpu as pltpu
from jax.sharding import PartitionSpec as P

MESH = pl.DeviceIdType.MESH
F32 = jnp.float32
BF16 = jnp.bfloat16

SIDE = 4
SUB = 8
FIRST = (0, 0, 1, 1, 3, 3, 3, 5, 6, 6, 6, 6, 6, 6, 6, 6)
CHUNKS = 2


def pick(table, index):
    value = jnp.int32(table[0])
    for position in range(1, len(table)):
        value = jnp.where(index == position, jnp.int32(table[position]), value)
    return value


def remote(src, dst, send_sem, recv_sem, device):
    return pltpu.make_async_remote_copy(
        src_ref=src,
        dst_ref=dst,
        send_sem=send_sem,
        recv_sem=recv_sem,
        device_id=device,
        device_id_type=MESH,
    )


def operator_kernel(
    q_hbm,
    k_hbm,
    v_hbm,
    res_hbm,
    dec_hbm,
    skip_hbm,
    w_hbm,
    out_ref,
    q_in,
    k_in,
    v_in,
    res,
    dec,
    skip,
    weight,
    xpad,
    kern,
    conv,
    gain,
    step8,
    state,
    carry,
    own_msg,
    pre_msg,
    got,
    gated,
    part,
    part_in,
    half_sum,
    half_in,
    in_sem,
    e_send,
    p_send,
    c_recv,
    r1_send,
    r1_recv,
    r2_send,
    r2_recv,
):
    blocks = len(FIRST)
    tokens, channels = k_in.shape
    groups = tokens // SUB
    modes = res.shape[0]
    width = part.shape[3]
    z = lax.axis_index("ctx")
    tp = lax.axis_index("tp")
    x, y = tp // SIDE, tp % SIDE

    def line(axis, shift):
        if axis == 0:
            return {"tp": (x + shift) % SIDE * SIDE + y}
        return {"tp": x * SIDE + (y + shift) % SIDE}

    first = pick(FIRST, z)
    fan_out = pick(
        [sum(FIRST[j] <= i < j for j in range(blocks)) for i in range(blocks)], z
    )
    sends_prefix = functools.reduce(
        jnp.logical_or, [z == i for i in sorted(set(FIRST[1:]))]
    )

    barrier = pltpu.get_barrier_semaphore()
    for shift in range(1, SIDE):
        for axis in (0, 1):
            pl.semaphore_signal(
                barrier, inc=1, device_id=line(axis, shift), device_id_type=MESH
            )

    @pl.loop(first, z)
    def _(source):
        pl.semaphore_signal(
            barrier, inc=1, device_id={"ctx": source}, device_id_type=MESH
        )

    loads = [
        pltpu.make_async_copy(src, dst, in_sem.at[i])
        for i, (src, dst) in enumerate(
            (
                (k_hbm, k_in),
                (v_hbm, v_in),
                (dec_hbm, dec),
                (res_hbm, res),
                (q_hbm, q_in),
                (skip_hbm, skip),
                (w_hbm, weight),
            )
        )
    ]
    for load in loads:
        load.start()
    for load in loads[:4]:
        load.wait()

    xpad[pl.ds(0, SUB), :] = jnp.zeros((SUB, channels), F32)
    xpad[pl.ds(SUB, tokens), :] = k_in[...].astype(F32) * v_in[...].astype(F32)

    row = lax.broadcasted_iota(jnp.int32, (SUB, channels), 0).astype(F32)
    for s in range(modes):
        rate = jnp.broadcast_to(dec[pl.ds(s, 1), :], (SUB, channels))
        amp = jnp.broadcast_to(res[pl.ds(s, 1), :], (SUB, channels)) * jnp.sqrt(
            2.0 * rate
        )
        a8 = jnp.exp(-float(SUB) * rate)
        step8[s] = a8
        gain[s] = amp * jnp.exp(-rate * row)
        total = xpad[pl.ds(SUB, SUB), :]
        for m in range(1, groups):
            total = total * a8 + xpad[pl.ds(SUB * (m + 1), SUB), :]
        total = total * jnp.exp(rate * (row - float(SUB - 1)))
        state[pl.ds(s, 1), :] = jnp.sum(total, axis=0, keepdims=True)
    own_msg[...] = state[...].astype(BF16)
    decay_block = jnp.exp(-float(tokens) * dec[...])

    pl.semaphore_wait(barrier, 2 * (SIDE - 1) + fan_out)

    for j in range(1, blocks):

        @pl.when(jnp.logical_and(z > FIRST[j], z < j))
        def _():
            remote(
                own_msg, got.at[z], e_send.at[j], c_recv.at[z], {"ctx": jnp.int32(j)}
            ).start()

    def receive_carry():
        carry[...] = jnp.zeros_like(carry)

        @pl.loop(first, z)
        def _(source):
            remote(
                own_msg, got.at[source], e_send.at[0], c_recv.at[source], {"ctx": z}
            ).wait_recv()
            carry[...] = carry[...] * decay_block + got[source].astype(F32)

    @pl.when(sends_prefix)
    def _():
        receive_carry()
        pre_msg[...] = (state[...] + decay_block * carry[...]).astype(BF16)
        for j in range(1, blocks):

            @pl.when(z == FIRST[j])
            def _():
                remote(
                    pre_msg,
                    got.at[z],
                    p_send.at[j],
                    c_recv.at[z],
                    {"ctx": jnp.int32(j)},
                ).start()

    for half in range(2):
        lanes = pl.ds(half * (channels // 2), channels // 2)
        base = [gain[s, :, lanes] for s in range(modes)]
        for m in range(groups):
            kern[pl.ds(SUB * m, SUB), lanes] = sum(base[1:], base[0])
            if m + 1 < groups:
                base = [b * step8[s, :, lanes] for s, b in enumerate(base)]
    loads[5].wait()
    conv[...] = jnp.broadcast_to(skip[...], (tokens, channels)) * xpad[pl.ds(SUB, tokens), :]
    for m in range(groups):
        rows = tokens - SUB * m
        conv[pl.ds(SUB * m, rows), :] += sum(
            jnp.broadcast_to(kern[pl.ds(SUB * m + f, 1), :], (rows, channels))
            * xpad[pl.ds(SUB - f, rows), :]
            for f in range(SUB)
        )
    loads[4].wait()

    @pl.when(jnp.logical_not(sends_prefix))
    def _():
        receive_carry()

    for half in range(2):
        lanes = pl.ds(half * (channels // 2), channels // 2)
        base = []
        for s in range(modes):
            a1 = jnp.exp(-dec[pl.ds(s, 1), lanes])
            base.append(
                gain[s, :, lanes]
                * jnp.broadcast_to(a1 * carry[pl.ds(s, 1), lanes], (SUB, channels // 2))
            )
        for m in range(groups):
            here = pl.ds(SUB * m, SUB)
            conv[here, lanes] += sum(base[1:], base[0])
            if m + 1 < groups:
                base = [b * step8[s, :, lanes] for s, b in enumerate(base)]
    product = q_in[...].astype(F32) * conv[...]
    gated[0] = product.astype(BF16)
    gated[1] = jnp.concatenate(
        [
            product[SUB * (SIDE * i + j) : SUB * (SIDE * i + j + 1)]
            for j in range(SIDE)
            for i in range(SIDE)
        ],
        axis=0,
    ).astype(BF16)

    loads[6].wait()
    place = (x, y)
    band = SIDE * SUB
    order = (2, 1, 3)

    def first_copy(c, h, shift):
        target = (place[h] + shift) % SIDE
        return remote(
            part.at[c, h, pl.ds(pl.multiple_of(target * band, band), band)],
            part_in.at[c, h, shift - 1],
            r1_send.at[c, h, shift - 1],
            r1_recv.at[c, h, shift - 1],
            line(h, shift),
        )

    def second_copy(c, h, shift):
        target = (place[1 - h] + shift) % SIDE
        return remote(
            half_sum.at[c, h, target],
            half_in.at[c, h, shift - 1],
            r2_send.at[c, h, shift - 1],
            r2_recv.at[c, h, shift - 1],
            line(1 - h, shift),
        )

    for c in range(CHUNKS):
        for h in range(2):
            columns = pl.ds((h * CHUNKS + c) * width, width)
            part[c, h] = jnp.dot(
                gated[h], weight[:, columns], preferred_element_type=F32
            ).astype(BF16)
            for shift in order:
                first_copy(c, h, shift).start()

    for c in range(CHUNKS):
        for h in range(2):
            mine = pl.ds(pl.multiple_of(place[h] * band, band), band)
            total = part[c, h, mine].astype(F32)
            for shift in order:
                first_copy(c, h, shift).wait_recv()
                total = total + part_in[c, h, shift - 1].astype(F32)
            for i in range(SIDE):
                rows = total[SUB * i : SUB * (i + 1)]
                half_sum[c, h, i] = jnp.concatenate(
                    [rows[:, : width // 2], rows[:, width // 2 :]], axis=0
                ).astype(BF16)
            for shift in order:
                second_copy(c, h, shift).start()

    for c in range(CHUNKS):
        for h in range(2):
            total = half_sum[c, h, place[1 - h]].astype(F32)
            for shift in order:
                second_copy(c, h, shift).wait_recv()
                total = total + half_in[c, h, shift - 1].astype(F32)
            start = (h * CHUNKS + c) * width
            out_ref[:, pl.ds(start, width // 2)] = total[:SUB].astype(BF16)
            out_ref[:, pl.ds(start + width // 2, width // 2)] = total[SUB:].astype(BF16)

    for c in range(CHUNKS):
        for h in range(2):
            for shift in order:
                first_copy(c, h, shift).wait_send()
                second_copy(c, h, shift).wait_send()
    for j in range(1, blocks):

        @pl.when(jnp.logical_and(z > FIRST[j], z < j))
        def _():
            remote(
                own_msg, got.at[z], e_send.at[j], c_recv.at[z], {"ctx": jnp.int32(j)}
            ).wait_send()

        @pl.when(z == FIRST[j])
        def _():
            remote(
                pre_msg, got.at[z], p_send.at[j], c_recv.at[z], {"ctx": jnp.int32(j)}
            ).wait_send()


def on_device(queries, keys, values, residues, decays, skip, out_weight):
    tokens, channels = keys.shape
    modes = residues.shape[1]
    features = out_weight.shape[1]
    blocks = len(FIRST)
    width = features // (2 * CHUNKS)
    band = SIDE * SUB
    hbm = pl.BlockSpec(memory_space=pltpu.HBM)
    dma = pltpu.SemaphoreType.DMA
    return pl.pallas_call(
        operator_kernel,
        out_shape=jax.ShapeDtypeStruct((SUB, features), BF16),
        in_specs=[hbm] * 7,
        out_specs=pl.BlockSpec(memory_space=pltpu.VMEM),
        scratch_shapes=[
            pltpu.VMEM((tokens, channels), BF16),
            pltpu.VMEM((tokens, channels), BF16),
            pltpu.VMEM((tokens, channels), BF16),
            pltpu.VMEM((modes, channels), F32),
            pltpu.VMEM((modes, channels), F32),
            pltpu.VMEM((1, channels), F32),
            pltpu.VMEM((channels, features), BF16),
            pltpu.VMEM((tokens + SUB, channels), F32),
            pltpu.VMEM((tokens, channels), F32),
            pltpu.VMEM((tokens, channels), F32),
            pltpu.VMEM((modes, SUB, channels), F32),
            pltpu.VMEM((modes, SUB, channels), F32),
            pltpu.VMEM((modes, channels), F32),
            pltpu.VMEM((modes, channels), F32),
            pltpu.VMEM((modes, channels), BF16),
            pltpu.VMEM((modes, channels), BF16),
            pltpu.VMEM((blocks, modes, channels), BF16),
            pltpu.VMEM((2, tokens, channels), BF16),
            pltpu.VMEM((CHUNKS, 2, tokens, width), BF16),
            pltpu.VMEM((CHUNKS, 2, SIDE - 1, band, width), BF16),
            pltpu.VMEM((CHUNKS, 2, SIDE, 2 * SUB, width // 2), BF16),
            pltpu.VMEM((CHUNKS, 2, SIDE - 1, 2 * SUB, width // 2), BF16),
            dma((7,)),
            dma((blocks,)),
            dma((blocks,)),
            dma((blocks,)),
            dma((CHUNKS, 2, SIDE - 1)),
            dma((CHUNKS, 2, SIDE - 1)),
            dma((CHUNKS, 2, SIDE - 1)),
            dma((CHUNKS, 2, SIDE - 1)),
        ],
        compiler_params=pltpu.CompilerParams(
            collective_id=0, has_side_effects=True, vmem_limit_bytes=48 << 20
        ),
    )(
        queries,
        keys,
        values,
        residues.T,
        decays.T,
        skip.reshape(1, channels),
        out_weight,
    )


def solution(mesh):
    placed = (
        P(("dp", "ctx"), "tp"),
        P(("dp", "ctx"), "tp"),
        P(("dp", "ctx"), "tp"),
        P("tp", None),
        P("tp", None),
        P("tp"),
        P("tp", None),
    )
    return jax.shard_map(
        on_device,
        mesh=mesh,
        in_specs=placed,
        out_specs=P(("dp", "ctx", "tp"), None),
        check_vma=False,
    )
```

```python
import functools

import jax
import jax.numpy as jnp
from jax import lax
from jax.experimental import pallas as pl
from jax.experimental.pallas import tpu as pltpu
from jax.sharding import PartitionSpec as P

MESH = pl.DeviceIdType.MESH
F32 = jnp.float32
BF16 = jnp.bfloat16

SIDE = 4
SUB = 8
FIRST = (0, 0, 1, 1, 3, 3, 3, 5, 6, 6, 6, 6, 6, 6, 6, 6)
CHUNKS = 2


def pick(table, index):
    value = jnp.int32(table[0])
    for position in range(1, len(table)):
        value = jnp.where(index == position, jnp.int32(table[position]), value)
    return value


def remote(src, dst, send_sem, recv_sem, device):
    return pltpu.make_async_remote_copy(
        src_ref=src,
        dst_ref=dst,
        send_sem=send_sem,
        recv_sem=recv_sem,
        device_id=device,
        device_id_type=MESH,
    )


def operator_kernel(
    q_hbm,
    k_hbm,
    v_hbm,
    res_hbm,
    dec_hbm,
    skip_hbm,
    w_hbm,
    out_ref,
    q_in,
    k_in,
    v_in,
    res,
    dec,
    skip,
    weight,
    xpad,
    kern,
    conv,
    gain,
    step8,
    state,
    carry,
    own_msg,
    pre_msg,
    got,
    gated,
    part,
    part_in,
    half_sum,
    half_in,
    in_sem,
    e_send,
    p_send,
    c_recv,
    r1_send,
    r1_recv,
    r2_send,
    r2_recv,
):
    blocks = len(FIRST)
    tokens, channels = k_in.shape
    groups = tokens // SUB
    modes = res.shape[0]
    width = part.shape[3]
    z = lax.axis_index("ctx")
    tp = lax.axis_index("tp")
    x, y = tp // SIDE, tp % SIDE

    def line(axis, shift):
        if axis == 0:
            return {"tp": (x + shift) % SIDE * SIDE + y}
        return {"tp": x * SIDE + (y + shift) % SIDE}

    first = pick(FIRST, z)
    fan_out = pick(
        [sum(FIRST[j] <= i < j for j in range(blocks)) for i in range(blocks)], z
    )
    sends_prefix = functools.reduce(
        jnp.logical_or, [z == i for i in sorted(set(FIRST[1:]))]
    )

    barrier = pltpu.get_barrier_semaphore()
    for shift in range(1, SIDE):
        for axis in (0, 1):
            pl.semaphore_signal(
                barrier, inc=1, device_id=line(axis, shift), device_id_type=MESH
            )

    @pl.loop(first, z)
    def _(source):
        pl.semaphore_signal(
            barrier, inc=1, device_id={"ctx": source}, device_id_type=MESH
        )

    loads = [
        pltpu.make_async_copy(src, dst, in_sem.at[i])
        for i, (src, dst) in enumerate(
            (
                (k_hbm, k_in),
                (v_hbm, v_in),
                (dec_hbm, dec),
                (res_hbm, res),
                (q_hbm, q_in),
                (skip_hbm, skip),
                (w_hbm, weight),
            )
        )
    ]
    for load in loads:
        load.start()
    for load in loads[:4]:
        load.wait()

    xpad[pl.ds(0, SUB), :] = jnp.zeros((SUB, channels), F32)
    xpad[pl.ds(SUB, tokens), :] = k_in[...].astype(F32) * v_in[...].astype(F32)

    row = lax.broadcasted_iota(jnp.int32, (SUB, channels), 0).astype(F32)
    for s in range(modes):
        rate = jnp.broadcast_to(dec[pl.ds(s, 1), :], (SUB, channels))
        amp = jnp.broadcast_to(res[pl.ds(s, 1), :], (SUB, channels)) * jnp.sqrt(
            2.0 * rate
        )
        a8 = jnp.exp(-float(SUB) * rate)
        step8[s] = a8
        gain[s] = amp * jnp.exp(-rate * row)
        total = xpad[pl.ds(SUB, SUB), :]
        for m in range(1, groups):
            total = total * a8 + xpad[pl.ds(SUB * (m + 1), SUB), :]
        total = total * jnp.exp(rate * (row - float(SUB - 1)))
        state[pl.ds(s, 1), :] = jnp.sum(total, axis=0, keepdims=True)
    own_msg[...] = state[...].astype(BF16)
    decay_block = jnp.exp(-float(tokens) * dec[...])

    pl.semaphore_wait(barrier, 2 * (SIDE - 1) + fan_out)

    for j in range(1, blocks):

        @pl.when(jnp.logical_and(z > FIRST[j], z < j))
        def _():
            remote(
                own_msg, got.at[z], e_send.at[j], c_recv.at[z], {"ctx": jnp.int32(j)}
            ).start()

    def receive_carry():
        carry[...] = jnp.zeros_like(carry)

        @pl.loop(first, z)
        def _(source):
            remote(
                own_msg, got.at[source], e_send.at[0], c_recv.at[source], {"ctx": z}
            ).wait_recv()
            carry[...] = carry[...] * decay_block + got[source].astype(F32)

    @pl.when(sends_prefix)
    def _():
        receive_carry()
        pre_msg[...] = (state[...] + decay_block * carry[...]).astype(BF16)
        for j in range(1, blocks):

            @pl.when(z == FIRST[j])
            def _():
                remote(
                    pre_msg,
                    got.at[z],
                    p_send.at[j],
                    c_recv.at[z],
                    {"ctx": jnp.int32(j)},
                ).start()

    for half in range(2):
        lanes = pl.ds(half * (channels // 2), channels // 2)
        base = [gain[s, :, lanes] for s in range(modes)]
        for m in range(groups):
            kern[pl.ds(SUB * m, SUB), lanes] = sum(base[1:], base[0])
            if m + 1 < groups:
                base = [b * step8[s, :, lanes] for s, b in enumerate(base)]
    loads[5].wait()
    conv[...] = jnp.broadcast_to(skip[...], (tokens, channels)) * xpad[pl.ds(SUB, tokens), :]
    for m in range(groups):
        rows = tokens - SUB * m
        conv[pl.ds(SUB * m, rows), :] += sum(
            jnp.broadcast_to(kern[pl.ds(SUB * m + f, 1), :], (rows, channels))
            * xpad[pl.ds(SUB - f, rows), :]
            for f in range(SUB)
        )
    loads[4].wait()

    @pl.when(jnp.logical_not(sends_prefix))
    def _():
        receive_carry()

    for half in range(2):
        lanes = pl.ds(half * (channels // 2), channels // 2)
        base = []
        for s in range(modes):
            a1 = jnp.exp(-dec[pl.ds(s, 1), lanes])
            base.append(
                gain[s, :, lanes]
                * jnp.broadcast_to(a1 * carry[pl.ds(s, 1), lanes], (SUB, channels // 2))
            )
        for m in range(groups):
            here = pl.ds(SUB * m, SUB)
            conv[here, lanes] += sum(base[1:], base[0])
            if m + 1 < groups:
                base = [b * step8[s, :, lanes] for s, b in enumerate(base)]
    product = q_in[...].astype(F32) * conv[...]
    gated[0] = product.astype(BF16)
    gated[1] = jnp.concatenate(
        [
            product[SUB * (SIDE * i + j) : SUB * (SIDE * i + j + 1)]
            for j in range(SIDE)
            for i in range(SIDE)
        ],
        axis=0,
    ).astype(BF16)

    loads[6].wait()
    place = (x, y)
    band = SIDE * SUB
    order = (2, 1, 3)

    def first_copy(c, h, shift):
        target = (place[h] + shift) % SIDE
        return remote(
            part.at[c, h, pl.ds(pl.multiple_of(target * band, band), band)],
            part_in.at[c, h, shift - 1],
            r1_send.at[c, h, shift - 1],
            r1_recv.at[c, h, shift - 1],
            line(h, shift),
        )

    def second_copy(c, h, shift):
        target = (place[1 - h] + shift) % SIDE
        return remote(
            half_sum.at[c, h, target],
            half_in.at[c, h, shift - 1],
            r2_send.at[c, h, shift - 1],
            r2_recv.at[c, h, shift - 1],
            line(1 - h, shift),
        )

    for c in range(CHUNKS):
        for h in range(2):
            columns = pl.ds((h * CHUNKS + c) * width, width)
            part[c, h] = jnp.dot(
                gated[h], weight[:, columns], preferred_element_type=F32
            ).astype(BF16)
            for shift in order:
                first_copy(c, h, shift).start()

    for c in range(CHUNKS):
        for h in range(2):
            mine = pl.ds(pl.multiple_of(place[h] * band, band), band)
            total = part[c, h, mine].astype(F32)
            for shift in order:
                first_copy(c, h, shift).wait_recv()
                total = total + part_in[c, h, shift - 1].astype(F32)
            for i in range(SIDE):
                rows = total[SUB * i : SUB * (i + 1)]
                half_sum[c, h, i] = jnp.concatenate(
                    [rows[:, : width // 2], rows[:, width // 2 :]], axis=0
                ).astype(BF16)
            for shift in order:
                second_copy(c, h, shift).start()

    for c in range(CHUNKS):
        for h in range(2):
            total = half_sum[c, h, place[1 - h]].astype(F32)
            for shift in order:
                second_copy(c, h, shift).wait_recv()
                total = total + half_in[c, h, shift - 1].astype(F32)
            start = (h * CHUNKS + c) * width
            out_ref[:, pl.ds(start, width // 2)] = total[:SUB].astype(BF16)
            out_ref[:, pl.ds(start + width // 2, width // 2)] = total[SUB:].astype(BF16)

    for c in range(CHUNKS):
        for h in range(2):
            for shift in order:
                first_copy(c, h, shift).wait_send()
                second_copy(c, h, shift).wait_send()
    for j in range(1, blocks):

        @pl.when(jnp.logical_and(z > FIRST[j], z < j))
        def _():
            remote(
                own_msg, got.at[z], e_send.at[j], c_recv.at[z], {"ctx": jnp.int32(j)}
            ).wait_send()

        @pl.when(z == FIRST[j])
        def _():
            remote(
                pre_msg, got.at[z], p_send.at[j], c_recv.at[z], {"ctx": jnp.int32(j)}
            ).wait_send()


def on_device(queries, keys, values, residues, decays, skip, out_weight):
    tokens, channels = keys.shape
    modes = residues.shape[1]
    features = out_weight.shape[1]
    blocks = len(FIRST)
    width = features // (2 * CHUNKS)
    band = SIDE * SUB
    hbm = pl.BlockSpec(memory_space=pltpu.HBM)
    dma = pltpu.SemaphoreType.DMA
    return pl.pallas_call(
        operator_kernel,
        out_shape=pltpu.VMEM((SUB, features), BF16),
        in_specs=[hbm] * 7,
        out_specs=pl.BlockSpec(memory_space=pltpu.VMEM),
        scratch_shapes=[
            pltpu.VMEM((tokens, channels), BF16),
            pltpu.VMEM((tokens, channels), BF16),
            pltpu.VMEM((tokens, channels), BF16),
            pltpu.VMEM((modes, channels), F32),
            pltpu.VMEM((modes, channels), F32),
            pltpu.VMEM((1, channels), F32),
            pltpu.VMEM((channels, features), BF16),
            pltpu.VMEM((tokens + SUB, channels), F32),
            pltpu.VMEM((tokens, channels), F32),
            pltpu.VMEM((tokens, channels), F32),
            pltpu.VMEM((modes, SUB, channels), F32),
            pltpu.VMEM((modes, SUB, channels), F32),
            pltpu.VMEM((modes, channels), F32),
            pltpu.VMEM((modes, channels), F32),
            pltpu.VMEM((modes, channels), BF16),
            pltpu.VMEM((modes, channels), BF16),
            pltpu.VMEM((blocks, modes, channels), BF16),
            pltpu.VMEM((2, tokens, channels), BF16),
            pltpu.VMEM((CHUNKS, 2, tokens, width), BF16),
            pltpu.VMEM((CHUNKS, 2, SIDE - 1, band, width), BF16),
            pltpu.VMEM((CHUNKS, 2, SIDE, 2 * SUB, width // 2), BF16),
            pltpu.VMEM((CHUNKS, 2, SIDE - 1, 2 * SUB, width // 2), BF16),
            dma((7,)),
            dma((blocks,)),
            dma((blocks,)),
            dma((blocks,)),
            dma((CHUNKS, 2, SIDE - 1)),
            dma((CHUNKS, 2, SIDE - 1)),
            dma((CHUNKS, 2, SIDE - 1)),
            dma((CHUNKS, 2, SIDE - 1)),
        ],
        compiler_params=pltpu.CompilerParams(
            collective_id=0, has_side_effects=True, vmem_limit_bytes=60 << 20
        ),
    )(
        queries,
        keys,
        values,
        residues.T,
        decays.T,
        skip.reshape(1, channels),
        out_weight,
    )


def solution(mesh):
    placed = (
        P(("dp", "ctx"), "tp"),
        P(("dp", "ctx"), "tp"),
        P(("dp", "ctx"), "tp"),
        P("tp", None),
        P("tp", None),
        P("tp"),
        P("tp", None),
    )
    return jax.shard_map(
        on_device,
        mesh=mesh,
        in_specs=placed,
        out_specs=P(("dp", "ctx", "tp"), None),
        check_vma=False,
    )
```

```python
import functools

import jax
import jax.numpy as jnp
from jax import lax
from jax.experimental import pallas as pl
from jax.experimental.pallas import tpu as pltpu
from jax.sharding import PartitionSpec as P

MESH = pl.DeviceIdType.MESH
F32 = jnp.float32
BF16 = jnp.bfloat16

SIDE = 4
SUB = 8
HEAD = (0, 0, 1, 0, 3, 3, 3, 6, 6, 6, 6, 6, 1, 1, 1, 1)
HUB, HUB_HEAD, HUB_LAST, HUB_TO = 1, 3, 6, (12, 13, 14, 15)
PAIR = 8
LATE = {HUB: HUB_TO, 6: (8, 9, 10, 11)}
CHUNKS = 2


def pick(table, index):
    value = jnp.int32(table[0])
    for position in range(1, len(table)):
        value = jnp.where(index == position, jnp.int32(table[position]), value)
    return value


def remote(src, dst, send_sem, recv_sem, device):
    return pltpu.make_async_remote_copy(
        src_ref=src,
        dst_ref=dst,
        send_sem=send_sem,
        recv_sem=recv_sem,
        device_id=device,
        device_id_type=MESH,
    )


def operator_kernel(
    q_hbm,
    k_hbm,
    v_hbm,
    res_hbm,
    dec_hbm,
    skip_hbm,
    w_hbm,
    out_ref,
    q_in,
    k_in,
    v_in,
    res,
    dec,
    skip,
    weight,
    xpad,
    kern,
    conv,
    gain,
    step8,
    state,
    carry,
    own_msg,
    pre_msg,
    hub_msg,
    got,
    gated,
    part,
    part_in,
    relay_in,
    relay_out,
    half_sum,
    half_in,
    in_sem,
    e_send,
    p_send,
    c_recv,
    a_send,
    a_recv,
    r1_send,
    r1_recv,
    r2_send,
    r2_recv,
    ready,
):
    blocks = len(HEAD)
    tokens, channels = k_in.shape
    groups = tokens // SUB
    modes = res.shape[0]
    width = part.shape[3]
    z = lax.axis_index("ctx")
    tp = lax.axis_index("tp")
    core = lax.axis_index("dp")
    x, y = tp // SIDE, tp % SIDE

    def line(axis, shift):
        if axis == 0:
            return {"tp": (x + shift) % SIDE * SIDE + y}
        return {"tp": x * SIDE + (y + shift) % SIDE}

    plain = {j: [] for j in range(blocks)}
    whole = {j: [] for j in range(blocks)}
    for j in range(1, blocks):
        start = HEAD[j] + 1 if j <= PAIR else PAIR + 1
        plain[j] += list(range(start, j))
        if j > PAIR:
            whole[j].append(PAIR)
        if j not in HUB_TO:
            whole[j].append(HEAD[j])
    plain[HUB] += list(range(HUB_HEAD + 1, HUB_LAST + 1))
    whole[HUB].append(HUB_HEAD)
    late = {j: k for k, group in LATE.items() for j in group}
    greeted = {
        j: [k for k in plain[j] + whole[j] if late.get(j) != k] for j in range(blocks)
    }
    expected = pick(
        [
            sum(i in greeted[j] for j in range(blocks)) + (i in late)
            for i in range(blocks)
        ],
        z,
    )

    def among(members):
        return functools.reduce(jnp.logical_or, [z == i for i in sorted(members)])

    heads = among({k for j in range(1, blocks) for k in whole[j]} - {PAIR})
    barrier = pltpu.get_barrier_semaphore()

    for source in range(blocks):
        if any(source in greeted[j] for j in range(blocks)):

            @pl.when(among([j for j in range(blocks) if source in greeted[j]]))
            def _():
                pl.semaphore_signal(
                    barrier,
                    inc=1,
                    device_id={"ctx": jnp.int32(source)},
                    device_id_type=MESH,
                )

    for source, group in LATE.items():

        @pl.when(z == source)
        def _():
            for j in group:
                pl.semaphore_signal(
                    barrier,
                    inc=1,
                    device_id={"ctx": jnp.int32(j)},
                    device_id_type=MESH,
                )

    for shift in (2, 1, 3):
        for axis in (0, 1):
            pl.semaphore_signal(
                barrier, inc=1, device_id=line(axis, shift), device_id_type=MESH
            )

    loads = [
        pltpu.make_async_copy(src, dst, in_sem.at[i])
        for i, (src, dst) in enumerate(
            (
                (k_hbm, k_in),
                (v_hbm, v_in),
                (dec_hbm, dec),
                (res_hbm, res),
                (q_hbm, q_in),
                (skip_hbm, skip),
                (w_hbm, weight),
            )
        )
    ]
    for load in loads:
        load.start()
    for load in loads[:4]:
        load.wait()

    xpad[pl.ds(0, SUB), :] = jnp.zeros((SUB, channels), F32)
    xpad[pl.ds(SUB, tokens), :] = k_in[...].astype(F32) * v_in[...].astype(F32)

    row = lax.broadcasted_iota(jnp.int32, (SUB, channels), 0).astype(F32)
    for s in range(modes):
        rate = jnp.broadcast_to(dec[pl.ds(s, 1), :], (SUB, channels))
        amp = jnp.broadcast_to(res[pl.ds(s, 1), :], (SUB, channels)) * jnp.sqrt(
            2.0 * rate
        )
        a8 = jnp.exp(-float(SUB) * rate)
        step8[s] = a8
        gain[s] = amp * jnp.exp(-rate * row)
        total = xpad[pl.ds(SUB, SUB), :]
        for m in range(1, groups):
            total = total * a8 + xpad[pl.ds(SUB * (m + 1), SUB), :]
        total = total * jnp.exp(rate * (row - float(SUB - 1)))
        state[pl.ds(s, 1), :] = jnp.sum(total, axis=0, keepdims=True)
    own_msg[...] = state[...].astype(BF16)
    decay_block = jnp.exp(-float(tokens) * dec[...])

    pl.semaphore_wait(barrier, 2 * (SIDE - 1) + expected)
    for source, group in LATE.items():

        @pl.when(among(group))
        def _():
            pl.semaphore_signal(
                ready,
                inc=1,
                device_id={"ctx": jnp.int32(source)},
                device_id_type=MESH,
            )

    def message(buffer, sems, j):
        return remote(
            buffer, got.at[z], sems.at[j], c_recv.at[z], {"ctx": jnp.int32(j)}
        )

    def arrived(source):
        remote(
            own_msg, got.at[source], e_send.at[0], c_recv.at[source], {"ctx": z}
        ).wait_recv()

    for j in reversed(range(1, blocks)):
        if plain[j]:

            @pl.when(among(plain[j]))
            def _():
                message(own_msg, e_send, j).start()

    def receive_carry():
        carry[...] = jnp.zeros_like(carry)

        @pl.when(z > 0)
        def _():
            head = pick(HEAD, z)
            arrived(head)
            carry[...] = got[head].astype(F32)

        @pl.when(z > PAIR)
        def _():
            arrived(jnp.int32(PAIR))
            carry[...] = carry[...] * decay_block * decay_block + got[PAIR].astype(F32)

        @pl.loop(jnp.where(z > PAIR, PAIR + 1, pick(HEAD, z) + 1), z)
        def _(source):
            @pl.when(source != PAIR - 1)
            def _():
                arrived(source)

            carry[...] = carry[...] * decay_block + got[source].astype(F32)

    def send_whole(k, targets):
        for j in reversed(targets):
            message(pre_msg, p_send, j).start()

    @pl.when(z == PAIR)
    def _():
        arrived(jnp.int32(PAIR - 1))
        pre_msg[...] = (
            state[...] + decay_block * got[PAIR - 1].astype(F32)
        ).astype(BF16)
        send_whole(PAIR, [j for j in range(blocks) if PAIR in whole[j]])

    @pl.when(heads)
    def _():
        receive_carry()
        pre_msg[...] = (state[...] + decay_block * carry[...]).astype(BF16)
        for k in sorted({k for j in whole for k in whole[j]} - {PAIR}):

            @pl.when(z == k)
            def _():
                targets = [j for j in range(blocks) if k in whole[j]]
                send_whole(k, [j for j in targets if late.get(j) != k])
                if k in LATE and k != HUB:
                    pl.semaphore_wait(ready, len(LATE[k]))
                    send_whole(k, [j for j in targets if late.get(j) == k])

    def hub_step():
        @pl.when(z == HUB)
        def _():
            total = None
            for source in range(HUB_HEAD, HUB_LAST + 1):
                arrived(jnp.int32(source))
                block = got[source].astype(F32)
                total = block if total is None else total * decay_block + block
            hub_msg[...] = total.astype(BF16)
            pl.semaphore_wait(ready, len(HUB_TO))
            for j in reversed(HUB_TO):
                message(hub_msg, p_send, j).start()

    for half in range(2):
        lanes = pl.ds(half * (channels // 2), channels // 2)
        base = [gain[s, :, lanes] for s in range(modes)]
        for m in range(groups):
            kern[pl.ds(SUB * m, SUB), lanes] = sum(base[1:], base[0])
            if m + 1 < groups:
                base = [b * step8[s, :, lanes] for s, b in enumerate(base)]
    loads[5].wait()
    conv[...] = jnp.broadcast_to(skip[...], (tokens, channels)) * xpad[pl.ds(SUB, tokens), :]
    for m in range(groups):
        rows = tokens - SUB * m
        conv[pl.ds(SUB * m, rows), :] += sum(
            jnp.broadcast_to(kern[pl.ds(SUB * m + f, 1), :], (rows, channels))
            * xpad[pl.ds(SUB - f, rows), :]
            for f in range(SUB)
        )
    loads[4].wait()

    @pl.when(jnp.logical_not(heads))
    def _():
        receive_carry()

    for half in range(2):
        lanes = pl.ds(half * (channels // 2), channels // 2)
        base = []
        for s in range(modes):
            a1 = jnp.exp(-dec[pl.ds(s, 1), lanes])
            base.append(
                gain[s, :, lanes]
                * jnp.broadcast_to(a1 * carry[pl.ds(s, 1), lanes], (SUB, channels // 2))
            )
        for m in range(groups):
            here = pl.ds(SUB * m, SUB)
            conv[here, lanes] += sum(base[1:], base[0])
            if m + 1 < groups:
                base = [b * step8[s, :, lanes] for s, b in enumerate(base)]
    product = q_in[...].astype(F32) * conv[...]
    gated[0] = product.astype(BF16)
    gated[1] = jnp.concatenate(
        [
            product[SUB * (SIDE * i + j) : SUB * (SIDE * i + j + 1)]
            for j in range(SIDE)
            for i in range(SIDE)
        ],
        axis=0,
    ).astype(BF16)

    loads[6].wait()
    place = (x, y)
    band = SIDE * SUB
    cut = band // 2
    order = (2, 1, 3)
    pieces = [(c, h) for c in range(CHUNKS) for h in range(2)]

    def rows_of(c, h, shift, low=0, count=band):
        target = (place[h] + shift) % SIDE
        return part.at[c, h, pl.ds(pl.multiple_of(target * band + low, cut), count)]

    def project(c, h):
        columns = pl.ds((h * CHUNKS + c) * width, width)
        part[c, h] = jnp.dot(
            gated[h], weight[:, columns], preferred_element_type=F32
        ).astype(BF16)

    def first_copy(c, h, shift):
        return remote(
            rows_of(c, h, shift),
            part_in.at[c, h, shift - 1],
            r1_send.at[c, h, shift - 1],
            r1_recv.at[c, h, shift - 1],
            line(h, shift),
        )

    def opposite_copy(c, h, side):
        return remote(
            rows_of(c, h, 2, side * cut, cut),
            relay_in.at[c, h, side],
            a_send.at[c, h, side],
            a_recv.at[c, h, side],
            line(h, (1, SIDE - 1)[side]),
        )

    def direct_copy(c, h, side):
        low = (1 - side) * cut
        return remote(
            rows_of(c, h, (1, SIDE - 1)[side], low, cut),
            part_in.at[c, h, side, pl.ds(low, cut)],
            r1_send.at[c, h, side],
            r1_recv.at[c, h, side],
            line(h, (1, SIDE - 1)[side]),
        )

    def relay_copy(c, h, side):
        return remote(
            relay_out.at[c, h, side],
            part_in.at[c, h, side, pl.ds(side * cut, cut)],
            r1_send.at[c, h, 2 + side],
            r1_recv.at[c, h, 2 + side],
            line(h, (1, SIDE - 1)[side]),
        )

    def second_copy(c, h, shift):
        target = (place[1 - h] + shift) % SIDE
        return remote(
            half_sum.at[c, h, target],
            half_in.at[c, h, shift - 1],
            r2_send.at[c, h, shift - 1],
            r2_recv.at[c, h, shift - 1],
            line(1 - h, shift),
        )

    def second_phase(c, h, total):
        for i in range(SIDE):
            rows = total[SUB * i : SUB * (i + 1)]
            half_sum[c, h, i] = jnp.concatenate(
                [rows[:, : width // 2], rows[:, width // 2 :]], axis=0
            ).astype(BF16)
        for shift in order:
            second_copy(c, h, shift).start()

    @pl.when(core == 0)
    def _():
        for c in range(CHUNKS):
            for h in range(2):
                project(c, h)
                first_copy(c, h, 2).start()
            for h in range(2):
                for shift in (1, 3):
                    first_copy(c, h, shift).start()
        hub_step()
        for c, h in pieces:
            total = rows_of(c, h, 0)[...].astype(F32)
            for shift in order:
                first_copy(c, h, shift).wait_recv()
                total = total + part_in[c, h, shift - 1].astype(F32)
            second_phase(c, h, total)

    @pl.when(core == 1)
    def _():
        for c, h in pieces:
            project(c, h)
            for side in range(2):
                opposite_copy(c, h, side).start()
        for c, h in pieces:
            for side in range(2):
                direct_copy(c, h, side).start()
        hub_step()
        for c, h in pieces:
            for side in range(2):
                opposite_copy(c, h, side).wait_recv()
                mine = rows_of(c, h, (1, SIDE - 1)[side], side * cut, cut)
                relay_out[c, h, side] = (
                    mine[...].astype(F32) + relay_in[c, h, side].astype(F32)
                ).astype(BF16)
                relay_copy(c, h, side).start()
        for c, h in pieces:
            for side in range(2):
                direct_copy(c, h, side).wait_recv()
                relay_copy(c, h, side).wait_recv()
            second_phase(
                c,
                h,
                rows_of(c, h, 0)[...].astype(F32)
                + part_in[c, h, 0].astype(F32)
                + part_in[c, h, 1].astype(F32),
            )

    for c, h in pieces:
        total = half_sum[c, h, place[1 - h]].astype(F32)
        for shift in order:
            second_copy(c, h, shift).wait_recv()
            total = total + half_in[c, h, shift - 1].astype(F32)
        start = (h * CHUNKS + c) * width
        out_ref[:, pl.ds(start, width // 2)] = total[:SUB].astype(BF16)
        out_ref[:, pl.ds(start + width // 2, width // 2)] = total[SUB:].astype(BF16)

    @pl.when(core == 0)
    def _():
        for c, h in pieces:
            for shift in order:
                first_copy(c, h, shift).wait_send()

    @pl.when(core == 1)
    def _():
        for c, h in pieces:
            for side in range(2):
                opposite_copy(c, h, side).wait_send()
                direct_copy(c, h, side).wait_send()
                relay_copy(c, h, side).wait_send()

    for c, h in pieces:
        for shift in order:
            second_copy(c, h, shift).wait_send()
    for j in range(1, blocks):
        if plain[j]:

            @pl.when(among(plain[j]))
            def _():
                message(own_msg, e_send, j).wait_send()

        senders = whole[j] + ([HUB] if j in HUB_TO else [])
        if senders:

            @pl.when(among(senders))
            def _():
                message(pre_msg, p_send, j).wait_send()


def on_device(queries, keys, values, residues, decays, skip, out_weight):
    tokens, channels = keys.shape
    modes = residues.shape[1]
    features = out_weight.shape[1]
    blocks = len(HEAD)
    width = features // (2 * CHUNKS)
    band = SIDE * SUB
    hbm = pl.BlockSpec(memory_space=pltpu.HBM)
    dma = pltpu.SemaphoreType.DMA
    return pl.pallas_call(
        operator_kernel,
        out_shape=pltpu.VMEM((SUB, features), BF16),
        in_specs=[hbm] * 7,
        out_specs=pl.BlockSpec(memory_space=pltpu.VMEM),
        scratch_shapes=[
            pltpu.VMEM((tokens, channels), BF16),
            pltpu.VMEM((tokens, channels), BF16),
            pltpu.VMEM((tokens, channels), BF16),
            pltpu.VMEM((modes, channels), F32),
            pltpu.VMEM((modes, channels), F32),
            pltpu.VMEM((1, channels), F32),
            pltpu.VMEM((channels, features), BF16),
            pltpu.VMEM((tokens + SUB, channels), F32),
            pltpu.VMEM((tokens, channels), F32),
            pltpu.VMEM((tokens, channels), F32),
            pltpu.VMEM((modes, SUB, channels), F32),
            pltpu.VMEM((modes, SUB, channels), F32),
            pltpu.VMEM((modes, channels), F32),
            pltpu.VMEM((modes, channels), F32),
            pltpu.VMEM((modes, channels), BF16),
            pltpu.VMEM((modes, channels), BF16),
            pltpu.VMEM((modes, channels), BF16),
            pltpu.VMEM((blocks, modes, channels), BF16),
            pltpu.VMEM((2, tokens, channels), BF16),
            pltpu.VMEM((CHUNKS, 2, tokens, width), BF16),
            pltpu.VMEM((CHUNKS, 2, SIDE - 1, band, width), BF16),
            pltpu.VMEM((CHUNKS, 2, 2, band // 2, width), BF16),
            pltpu.VMEM((CHUNKS, 2, 2, band // 2, width), BF16),
            pltpu.VMEM((CHUNKS, 2, SIDE, 2 * SUB, width // 2), BF16),
            pltpu.VMEM((CHUNKS, 2, SIDE - 1, 2 * SUB, width // 2), BF16),
            dma((7,)),
            dma((blocks,)),
            dma((blocks,)),
            dma((blocks,)),
            dma((CHUNKS, 2, 2)),
            dma((CHUNKS, 2, 2)),
            dma((CHUNKS, 2, 4)),
            dma((CHUNKS, 2, 4)),
            dma((CHUNKS, 2, SIDE - 1)),
            dma((CHUNKS, 2, SIDE - 1)),
            pltpu.SemaphoreType.REGULAR,
        ],
        compiler_params=pltpu.CompilerParams(
            collective_id=0, has_side_effects=True, vmem_limit_bytes=60 << 20
        ),
    )(
        queries,
        keys,
        values,
        residues.T,
        decays.T,
        skip.reshape(1, channels),
        out_weight,
    )


def solution(mesh):
    placed = (
        P(("dp", "ctx"), "tp"),
        P(("dp", "ctx"), "tp"),
        P(("dp", "ctx"), "tp"),
        P("tp", None),
        P("tp", None),
        P("tp"),
        P("tp", None),
    )
    return jax.shard_map(
        on_device,
        mesh=mesh,
        in_specs=placed,
        out_specs=P(("dp", "ctx", "tp"), None),
        check_vma=False,
    )
```

```python
import functools

import jax
import jax.numpy as jnp
from jax import lax
from jax.experimental import pallas as pl
from jax.experimental.pallas import tpu as pltpu
from jax.sharding import PartitionSpec as P

MESH = pl.DeviceIdType.MESH
F32 = jnp.float32
BF16 = jnp.bfloat16

SIDE = 4
SUB = 8
HEAD = (0, 0, 1, 0, 3, 3, 3, 6, 6, 6, 6, 6, 0, 0, 0, 0)
HUB, HUB_HEAD, HUB_LAST, HUB_TO = 0, 3, 6, (12, 13, 14, 15)
PAIR = 8
LATE = {HUB: HUB_TO, 6: (8, 9, 10, 11)}
LEVELS = 2


def pick(table, index):
    value = jnp.int32(table[0])
    for position in range(1, len(table)):
        value = jnp.where(index == position, jnp.int32(table[position]), value)
    return value


def remote(src, dst, send_sem, recv_sem, device):
    return pltpu.make_async_remote_copy(
        src_ref=src,
        dst_ref=dst,
        send_sem=send_sem,
        recv_sem=recv_sem,
        device_id=device,
        device_id_type=MESH,
    )


def operator_kernel(
    q_hbm,
    k_hbm,
    v_hbm,
    res_hbm,
    dec_hbm,
    skip_hbm,
    w_hbm,
    out_ref,
    q_in,
    k_in,
    v_in,
    res,
    dec,
    skip,
    weight,
    xpad,
    kern,
    conv,
    gain,
    lead,
    step8,
    state,
    carry,
    own_msg,
    pre_msg,
    hub_msg,
    got,
    gated,
    part,
    part_in,
    relay_in,
    relay_out,
    half_sum,
    half_in,
    in_sem,
    e_send,
    p_send,
    c_recv,
    a_send,
    a_recv,
    r1_send,
    r1_recv,
    r2_send,
    r2_recv,
    ready,
):
    blocks = len(HEAD)
    tokens, channels = k_in.shape
    groups = tokens // SUB
    modes = res.shape[0]
    width = part.shape[4]
    split = width // 2
    z = lax.axis_index("ctx")
    tp = lax.axis_index("tp")
    core = lax.axis_index("dp")
    x, y = tp // SIDE, tp % SIDE

    def line(axis, shift):
        if axis == 0:
            return {"tp": (x + shift) % SIDE * SIDE + y}
        return {"tp": x * SIDE + (y + shift) % SIDE}

    plain = {j: [] for j in range(blocks)}
    whole = {j: [] for j in range(blocks)}
    for j in range(1, blocks):
        start = HEAD[j] + 1 if j <= PAIR else PAIR + 1
        plain[j] += list(range(start, j))
        if j > PAIR:
            whole[j].append(PAIR)
        if j not in HUB_TO:
            whole[j].append(HEAD[j])
    plain[HUB] += list(range(HUB_HEAD + 1, HUB_LAST + 1))
    whole[HUB].append(HUB_HEAD)
    late = {j: k for k, group in LATE.items() for j in group}
    greeted = {
        j: [k for k in plain[j] + whole[j] if late.get(j) != k] for j in range(blocks)
    }
    expected = pick(
        [
            sum(i in greeted[j] for j in range(blocks)) + (i in late)
            for i in range(blocks)
        ],
        z,
    )

    def among(members):
        return functools.reduce(jnp.logical_or, [z == i for i in sorted(members)])

    heads = among({k for j in range(blocks) for k in whole[j]} - {PAIR})
    barrier = pltpu.get_barrier_semaphore()

    for source in range(blocks):
        if any(source in greeted[j] for j in range(blocks)):

            @pl.when(among([j for j in range(blocks) if source in greeted[j]]))
            def _():
                pl.semaphore_signal(
                    barrier,
                    inc=1,
                    device_id={"ctx": jnp.int32(source)},
                    device_id_type=MESH,
                )

    for source, group in LATE.items():

        @pl.when(z == source)
        def _():
            for j in group:
                pl.semaphore_signal(
                    barrier,
                    inc=1,
                    device_id={"ctx": jnp.int32(j)},
                    device_id_type=MESH,
                )

    for shift in (2, 1, 3):
        for axis in (0, 1):
            pl.semaphore_signal(
                barrier, inc=1, device_id=line(axis, shift), device_id_type=MESH
            )

    loads = [
        pltpu.make_async_copy(src, dst, in_sem.at[i])
        for i, (src, dst) in enumerate(
            (
                (k_hbm, k_in),
                (v_hbm, v_in),
                (dec_hbm, dec),
                (res_hbm, res),
                (q_hbm, q_in),
                (skip_hbm, skip),
                (w_hbm, weight),
            )
        )
    ]
    for load in loads:
        load.start()
    for load in loads[:4]:
        load.wait()

    xpad[pl.ds(0, SUB), :] = jnp.zeros((SUB, channels), F32)
    xpad[pl.ds(SUB, tokens), :] = k_in[...].astype(F32) * v_in[...].astype(F32)

    row = lax.broadcasted_iota(jnp.int32, (SUB, channels), 0).astype(F32)
    for s in range(modes):
        rate = jnp.broadcast_to(dec[pl.ds(s, 1), :], (SUB, channels))
        amp = jnp.broadcast_to(res[pl.ds(s, 1), :], (SUB, channels)) * jnp.sqrt(
            2.0 * rate
        )
        a8 = jnp.exp(-float(SUB) * rate)
        step8[s] = a8
        gain[s] = amp * jnp.exp(-rate * row)
        lead[s] = amp * jnp.exp(-rate * (row + 1.0))
        total = xpad[pl.ds(SUB, SUB), :]
        for m in range(1, groups):
            total = total * a8 + xpad[pl.ds(SUB * (m + 1), SUB), :]
        total = total * jnp.exp(rate * (row - float(SUB - 1)))
        state[pl.ds(s, 1), :] = jnp.sum(total, axis=0, keepdims=True)
    own_msg[...] = state[...].astype(BF16)
    decay_block = jnp.exp(-float(tokens) * dec[...])

    pl.semaphore_wait(barrier, 2 * (SIDE - 1) + expected)
    for source, group in LATE.items():

        @pl.when(among(group))
        def _():
            pl.semaphore_signal(
                ready,
                inc=1,
                device_id={"ctx": jnp.int32(source)},
                device_id_type=MESH,
            )

    def message(buffer, sems, j):
        return remote(
            buffer, got.at[z], sems.at[j], c_recv.at[z], {"ctx": jnp.int32(j)}
        )

    def arrived(source):
        remote(
            own_msg, got.at[source], e_send.at[0], c_recv.at[source], {"ctx": z}
        ).wait_recv()

    for j in reversed(range(blocks)):
        if plain[j]:

            @pl.when(among(plain[j]))
            def _():
                message(own_msg, e_send, j).start()

    head = pick(HEAD, z)
    behind = jnp.where(z > PAIR, z - 1 - HUB_LAST, z - 1 - head)
    head_decay = jnp.exp(
        -float(tokens) * jnp.maximum(behind, 0).astype(F32) * dec[...]
    )
    pair_decay = jnp.exp(
        -float(tokens) * jnp.maximum(z - 1 - PAIR, 0).astype(F32) * dec[...]
    )

    def receive_carry():
        carry[...] = jnp.zeros_like(carry)

        @pl.loop(jnp.where(z > PAIR, PAIR, head) + 1, z)
        def _(source):
            @pl.when(source != PAIR - 1)
            def _():
                arrived(source)

            carry[...] = carry[...] * decay_block + got[source].astype(F32)

        @pl.when(z > PAIR)
        def _():
            arrived(jnp.int32(PAIR))
            carry[...] += pair_decay * got[PAIR].astype(F32)

        @pl.when(z > 0)
        def _():
            arrived(head)
            carry[...] += head_decay * got[head].astype(F32)

    def send_whole(k, targets):
        for j in reversed(targets):
            message(pre_msg, p_send, j).start()

    @pl.when(z == PAIR)
    def _():
        arrived(jnp.int32(PAIR - 1))
        pre_msg[...] = (
            state[...] + decay_block * got[PAIR - 1].astype(F32)
        ).astype(BF16)
        send_whole(PAIR, [j for j in range(blocks) if PAIR in whole[j]])

    @pl.when(heads)
    def _():
        receive_carry()
        pre_msg[...] = (state[...] + decay_block * carry[...]).astype(BF16)
        for k in sorted({k for j in whole for k in whole[j]} - {PAIR}):

            @pl.when(z == k)
            def _():
                targets = [j for j in range(blocks) if k in whole[j]]
                send_whole(k, [j for j in targets if late.get(j) != k])
                if k in LATE and k != HUB:
                    pl.semaphore_wait(ready, len(LATE[k]))
                    send_whole(k, [j for j in targets if late.get(j) == k])

    def hub_step():
        @pl.when(z == HUB)
        def _():
            total = None
            for source in range(HUB_HEAD, HUB_LAST + 1):
                arrived(jnp.int32(source))
                block = got[source].astype(F32)
                total = block if total is None else total * decay_block + block
            hub_msg[...] = total.astype(BF16)
            pl.semaphore_wait(ready, len(HUB_TO))
            for j in reversed(HUB_TO):
                message(hub_msg, p_send, j).start()

    for half in range(2):
        lanes = pl.ds(half * (channels // 2), channels // 2)
        base = [gain[s, :, lanes] for s in range(modes)]
        for m in range(groups):
            kern[pl.ds(SUB * m, SUB), lanes] = sum(base[1:], base[0])
            if m + 1 < groups:
                base = [b * step8[s, :, lanes] for s, b in enumerate(base)]
    loads[5].wait()
    conv[...] = jnp.broadcast_to(skip[...], (tokens, channels)) * xpad[pl.ds(SUB, tokens), :]
    for m in range(groups):
        rows = tokens - SUB * m
        conv[pl.ds(SUB * m, rows), :] += sum(
            jnp.broadcast_to(kern[pl.ds(SUB * m + f, 1), :], (rows, channels))
            * xpad[pl.ds(SUB - f, rows), :]
            for f in range(SUB)
        )
    loads[4].wait()

    @pl.when(jnp.logical_not(heads))
    def _():
        receive_carry()

    for half in range(2):
        lanes = pl.ds(half * (channels // 2), channels // 2)
        base = [
            lead[s, :, lanes]
            * jnp.broadcast_to(carry[pl.ds(s, 1), lanes], (SUB, channels // 2))
            for s in range(modes)
        ]
        for m in range(groups):
            here = pl.ds(SUB * m, SUB)
            conv[here, lanes] += sum(base[1:], base[0])
            if m + 1 < groups:
                base = [b * step8[s, :, lanes] for s, b in enumerate(base)]
    product = q_in[...].astype(F32) * conv[...]
    gated[0] = product.astype(BF16)
    gated[1] = jnp.concatenate(
        [
            product[SUB * (SIDE * i + j) : SUB * (SIDE * i + j + 1)]
            for j in range(SIDE)
            for i in range(SIDE)
        ],
        axis=0,
    ).astype(BF16)

    loads[6].wait()
    place = (x, y)
    band = SIDE * SUB
    cut = band // LEVELS
    order = (2, 1, 3)
    steps = (1, SIDE - 1)
    pieces = [(r, h) for r in range(LEVELS) for h in range(2)]

    def at(h, shift):
        return (place[h] + shift) % SIDE

    def project(h):
        for side in range(2):
            value = jnp.dot(
                gated[h],
                weight[:, pl.ds(h * width + side * split, split)],
                preferred_element_type=F32,
            ).astype(BF16)
            for r in range(LEVELS):
                for i in range(SIDE):
                    start = i * band + r * cut
                    part[r, h, i, :, pl.ds(side * split, split)] = value[
                        start : start + cut
                    ]

    def first_copy(r, h, shift):
        return remote(
            part.at[r, h, at(h, shift)],
            part_in.at[r, h, shift - 1],
            r1_send.at[r, h, shift - 1],
            r1_recv.at[r, h, shift - 1],
            line(h, shift),
        )

    def opposite_copy(r, h, side):
        return remote(
            part.at[r, h, at(h, 2), :, pl.ds(side * split, split)],
            relay_in.at[r, h, side],
            a_send.at[r, h, side],
            a_recv.at[r, h, side],
            line(h, steps[side]),
        )

    def direct_copy(r, h, side):
        columns = pl.ds((1 - side) * split, split)
        return remote(
            part.at[r, h, at(h, steps[side]), :, columns],
            part_in.at[r, h, side, :, columns],
            r1_send.at[r, h, side],
            r1_recv.at[r, h, side],
            line(h, steps[side]),
        )

    def relay_copy(r, h, side):
        return remote(
            relay_out.at[r, h, side],
            part_in.at[r, h, side, :, pl.ds(side * split, split)],
            r1_send.at[r, h, 2 + side],
            r1_recv.at[r, h, 2 + side],
            line(h, steps[side]),
        )

    def second_copy(h, target, shift):
        return remote(
            half_sum.at[h, target],
            half_in.at[h, shift - 1],
            r2_send.at[h, shift - 1],
            r2_recv.at[h, shift - 1],
            line(1 - h, shift),
        )

    def second_phase(r, h, total):
        for i in range(LEVELS):
            rows = total[SUB * i : SUB * (i + 1)]
            target = LEVELS * r + i
            half_sum[h, target] = jnp.concatenate(
                [rows[:, :split], rows[:, split:]], axis=0
            ).astype(BF16)

            @pl.when(place[1 - h] != target)
            def _():
                second_copy(h, target, (target - place[1 - h] + SIDE) % SIDE).start()

    @pl.when(core == 0)
    def _():
        for h in range(2):
            project(h)
            first_copy(0, h, 2).start()
        for r in range(LEVELS):
            for h in range(2):
                if r > 0:
                    first_copy(r, h, 2).start()
            for h in range(2):
                for shift in (1, 3):
                    first_copy(r, h, shift).start()
        hub_step()
        for r, h in pieces:
            total = part[r, h, place[h]].astype(F32)
            for shift in order:
                first_copy(r, h, shift).wait_recv()
                total = total + part_in[r, h, shift - 1].astype(F32)
            second_phase(r, h, total)

    @pl.when(core == 1)
    def _():
        for h in range(2):
            project(h)
            for r in range(LEVELS):
                for side in range(2):
                    opposite_copy(r, h, side).start()
        for r, h in pieces:
            for side in range(2):
                direct_copy(r, h, side).start()
        hub_step()
        for r, h in pieces:
            for side in range(2):
                opposite_copy(r, h, side).wait_recv()
                mine = part[r, h, at(h, steps[side]), :, pl.ds(side * split, split)]
                relay_out[r, h, side] = (
                    mine.astype(F32) + relay_in[r, h, side].astype(F32)
                ).astype(BF16)
                relay_copy(r, h, side).start()
        for r, h in pieces:
            for side in range(2):
                direct_copy(r, h, side).wait_recv()
                relay_copy(r, h, side).wait_recv()
            second_phase(
                r,
                h,
                part[r, h, place[h]].astype(F32)
                + part_in[r, h, 0].astype(F32)
                + part_in[r, h, 1].astype(F32),
            )

    @pl.when(core == 0)
    def _():
        for r, h in pieces:
            for shift in order:
                first_copy(r, h, shift).wait_send()

    @pl.when(core == 1)
    def _():
        for r, h in pieces:
            for side in range(2):
                opposite_copy(r, h, side).wait_send()
                direct_copy(r, h, side).wait_send()
                relay_copy(r, h, side).wait_send()

    for j in range(blocks):
        if plain[j]:

            @pl.when(among(plain[j]))
            def _():
                message(own_msg, e_send, j).wait_send()

        senders = whole[j] + ([HUB] if j in HUB_TO else [])
        if senders:

            @pl.when(among(senders))
            def _():
                message(pre_msg, p_send, j).wait_send()

    for h in range(2):
        for shift in order:
            second_copy(h, at(1 - h, shift), shift).wait_send()

    for h in range(2):
        total = half_sum[h, place[1 - h]].astype(F32)
        for shift in order:
            second_copy(h, place[1 - h], shift).wait_recv()
            total = total + half_in[h, shift - 1].astype(F32)
        for side in range(2):
            out_ref[:, pl.ds(h * width + side * split, split)] = total[
                SUB * side : SUB * (side + 1)
            ].astype(BF16)


def on_device(queries, keys, values, residues, decays, skip, out_weight):
    tokens, channels = keys.shape
    modes = residues.shape[1]
    features = out_weight.shape[1]
    blocks = len(HEAD)
    width = features // 2
    band = SIDE * SUB
    hbm = pl.BlockSpec(memory_space=pltpu.HBM)
    dma = pltpu.SemaphoreType.DMA
    return pl.pallas_call(
        operator_kernel,
        out_shape=pltpu.VMEM((SUB, features), BF16),
        in_specs=[hbm] * 7,
        out_specs=pl.BlockSpec(memory_space=pltpu.VMEM),
        scratch_shapes=[
            pltpu.VMEM((tokens, channels), BF16),
            pltpu.VMEM((tokens, channels), BF16),
            pltpu.VMEM((tokens, channels), BF16),
            pltpu.VMEM((modes, channels), F32),
            pltpu.VMEM((modes, channels), F32),
            pltpu.VMEM((1, channels), F32),
            pltpu.VMEM((channels, features), BF16),
            pltpu.VMEM((tokens + SUB, channels), F32),
            pltpu.VMEM((tokens, channels), F32),
            pltpu.VMEM((tokens, channels), F32),
            pltpu.VMEM((modes, SUB, channels), F32),
            pltpu.VMEM((modes, SUB, channels), F32),
            pltpu.VMEM((modes, SUB, channels), F32),
            pltpu.VMEM((modes, channels), F32),
            pltpu.VMEM((modes, channels), F32),
            pltpu.VMEM((modes, channels), BF16),
            pltpu.VMEM((modes, channels), BF16),
            pltpu.VMEM((modes, channels), BF16),
            pltpu.VMEM((blocks, modes, channels), BF16),
            pltpu.VMEM((2, tokens, channels), BF16),
            pltpu.VMEM((LEVELS, 2, SIDE, band // LEVELS, width), BF16),
            pltpu.VMEM((LEVELS, 2, SIDE - 1, band // LEVELS, width), BF16),
            pltpu.VMEM((LEVELS, 2, 2, band // LEVELS, width // 2), BF16),
            pltpu.VMEM((LEVELS, 2, 2, band // LEVELS, width // 2), BF16),
            pltpu.VMEM((2, SIDE, 2 * SUB, width // 2), BF16),
            pltpu.VMEM((2, SIDE - 1, 2 * SUB, width // 2), BF16),
            dma((7,)),
            dma((blocks,)),
            dma((blocks,)),
            dma((blocks,)),
            dma((LEVELS, 2, 2)),
            dma((LEVELS, 2, 2)),
            dma((LEVELS, 2, 4)),
            dma((LEVELS, 2, 4)),
            dma((2, SIDE - 1)),
            dma((2, SIDE - 1)),
            pltpu.SemaphoreType.REGULAR,
        ],
        compiler_params=pltpu.CompilerParams(
            collective_id=0, has_side_effects=True, vmem_limit_bytes=60 << 20
        ),
    )(
        queries,
        keys,
        values,
        residues.T,
        decays.T,
        skip.reshape(1, channels),
        out_weight,
    )


def solution(mesh):
    placed = (
        P(("dp", "ctx"), "tp"),
        P(("dp", "ctx"), "tp"),
        P(("dp", "ctx"), "tp"),
        P("tp", None),
        P("tp", None),
        P("tp"),
        P("tp", None),
    )
    return jax.shard_map(
        on_device,
        mesh=mesh,
        in_specs=placed,
        out_specs=P(("dp", "ctx", "tp"), None),
        check_vma=False,
    )
```

```python
import functools

import jax
import jax.numpy as jnp
from jax import lax
from jax.experimental import pallas as pl
from jax.experimental.pallas import tpu as pltpu
from jax.sharding import PartitionSpec as P

MESH = pl.DeviceIdType.MESH
F32 = jnp.float32
BF16 = jnp.bfloat16

SIDE = 4
SUB = 8
HEAD = (0, 0, 1, 0, 3, 3, 3, 6, 6, 6, 6, 6, 0, 0, 0, 0)
HUB, HUB_HEAD, HUB_LAST, HUB_TO = 0, 3, 6, (12, 13, 14, 15)
PAIR = 8
LATE = {HUB: HUB_TO, 6: (8, 9, 10, 11)}
LEVELS = 2


def pick(table, index):
    value = jnp.int32(table[0])
    for position in range(1, len(table)):
        value = jnp.where(index == position, jnp.int32(table[position]), value)
    return value


def remote(src, dst, send_sem, recv_sem, device):
    return pltpu.make_async_remote_copy(
        src_ref=src,
        dst_ref=dst,
        send_sem=send_sem,
        recv_sem=recv_sem,
        device_id=device,
        device_id_type=MESH,
    )


def operator_kernel(
    q_hbm,
    k_hbm,
    v_hbm,
    res_hbm,
    dec_hbm,
    skip_hbm,
    w_hbm,
    out_ref,
    q_in,
    k_in,
    v_in,
    res,
    dec,
    skip,
    weight,
    xpad,
    kern,
    conv,
    gain,
    lead,
    step8,
    state,
    carry,
    own_msg,
    pre_msg,
    hub_msg,
    got,
    gated,
    part,
    part_in,
    relay_in,
    relay_out,
    half_sum,
    half_in,
    in_sem,
    e_send,
    p_send,
    c_recv,
    a_send,
    a_recv,
    r1_send,
    r1_recv,
    r2_send,
    r2_recv,
    ready,
    turn,
):
    blocks = len(HEAD)
    tokens, channels = k_in.shape
    groups = tokens // SUB
    modes = res.shape[0]
    width = part.shape[4]
    split = width // 2
    z = lax.axis_index("ctx")
    tp = lax.axis_index("tp")
    core = lax.axis_index("dp")
    x, y = tp // SIDE, tp % SIDE

    def line(axis, shift):
        if axis == 0:
            return {"tp": (x + shift) % SIDE * SIDE + y}
        return {"tp": x * SIDE + (y + shift) % SIDE}

    plain = {j: [] for j in range(blocks)}
    whole = {j: [] for j in range(blocks)}
    for j in range(1, blocks):
        start = HEAD[j] + 1 if j <= PAIR else PAIR + 1
        plain[j] += list(range(start, j))
        if j > PAIR:
            whole[j].append(PAIR)
        if j not in HUB_TO:
            whole[j].append(HEAD[j])
    plain[HUB] += list(range(HUB_HEAD + 1, HUB_LAST + 1))
    whole[HUB].append(HUB_HEAD)
    late = {j: k for k, group in LATE.items() for j in group}
    greeted = {
        j: [k for k in plain[j] + whole[j] if late.get(j) != k] for j in range(blocks)
    }
    expected = pick(
        [
            sum(i in greeted[j] for j in range(blocks)) + (i in late)
            for i in range(blocks)
        ],
        z,
    )

    def among(members):
        members = sorted(members)
        spans = []
        for i in members:
            if spans and spans[-1][1] == i - 1:
                spans[-1][1] = i
            else:
                spans.append([i, i])
        return functools.reduce(
            jnp.logical_or,
            [
                z == low if low == high else jnp.logical_and(z >= low, z <= high)
                for low, high in spans
            ],
        )

    heads = among({k for j in range(blocks) for k in whole[j]} - {PAIR})
    barrier = pltpu.get_barrier_semaphore()

    for source in (*range(PAIR, blocks), *range(PAIR)):
        if any(source in greeted[j] for j in range(blocks)):

            @pl.when(among([j for j in range(blocks) if source in greeted[j]]))
            def _():
                pl.semaphore_signal(
                    barrier,
                    inc=1,
                    device_id={"ctx": jnp.int32(source)},
                    device_id_type=MESH,
                )

    for source, group in LATE.items():

        @pl.when(z == source)
        def _():
            for j in group:
                pl.semaphore_signal(
                    barrier,
                    inc=1,
                    device_id={"ctx": jnp.int32(j)},
                    device_id_type=MESH,
                )

    for shift in (2, 1, 3):
        for axis in (0, 1):
            pl.semaphore_signal(
                barrier, inc=1, device_id=line(axis, shift), device_id_type=MESH
            )

    @pl.when(core == 1)
    def _():
        pl.semaphore_signal(
            barrier, inc=1, device_id={"dp": jnp.int32(0)}, device_id_type=MESH
        )

    loads = [
        pltpu.make_async_copy(src, dst, in_sem.at[i])
        for i, (src, dst) in enumerate(
            (
                (k_hbm, k_in),
                (v_hbm, v_in),
                (dec_hbm, dec),
                (res_hbm, res),
                (q_hbm, q_in),
                (skip_hbm, skip),
                (w_hbm, weight),
            )
        )
    ]
    for load in loads:
        load.start()
    for load in loads[:4]:
        load.wait()

    xpad[pl.ds(0, SUB), :] = jnp.zeros((SUB, channels), F32)
    xpad[pl.ds(SUB, tokens), :] = k_in[...].astype(F32) * v_in[...].astype(F32)

    row = lax.broadcasted_iota(jnp.int32, (SUB, channels), 0).astype(F32)
    for s in range(modes):
        rate = jnp.broadcast_to(dec[pl.ds(s, 1), :], (SUB, channels))
        amp = jnp.broadcast_to(res[pl.ds(s, 1), :], (SUB, channels)) * jnp.sqrt(
            2.0 * rate
        )
        a8 = jnp.exp(-float(SUB) * rate)
        step8[s] = a8
        gain[s] = amp * jnp.exp(-rate * row)
        lead[s] = amp * jnp.exp(-rate * (row + 1.0))
        total = xpad[pl.ds(SUB, SUB), :]
        for m in range(1, groups):
            total = total * a8 + xpad[pl.ds(SUB * (m + 1), SUB), :]
        total = total * jnp.exp(rate * (row - float(SUB - 1)))
        state[pl.ds(s, 1), :] = jnp.sum(total, axis=0, keepdims=True)
    own_msg[...] = state[...].astype(BF16)
    decay_block = jnp.exp(-float(tokens) * dec[...])

    pl.semaphore_wait(barrier, 2 * (SIDE - 1) + expected + 1 - core)
    for source, group in LATE.items():

        @pl.when(among(group))
        def _():
            pl.semaphore_signal(
                ready,
                inc=1,
                device_id={"ctx": jnp.int32(source)},
                device_id_type=MESH,
            )

    def message(buffer, sems, j):
        return remote(
            buffer, got.at[z], sems.at[j], c_recv.at[z], {"ctx": jnp.int32(j)}
        )

    def arrived(source):
        remote(
            own_msg, got.at[source], e_send.at[0], c_recv.at[source], {"ctx": z}
        ).wait_recv()

    def send_whole(k, targets):
        for j in reversed(targets):
            message(pre_msg, p_send, j).start()

    @pl.when(z == PAIR)
    def _():
        arrived(jnp.int32(PAIR - 1))
        pre_msg[...] = (
            state[...] + decay_block * got[PAIR - 1].astype(F32)
        ).astype(BF16)
        send_whole(PAIR, [j for j in range(blocks) if PAIR in whole[j]])

    for j in reversed(range(blocks)):
        if plain[j]:

            @pl.when(among(plain[j]))
            def _():
                message(own_msg, e_send, j).start()

    head = pick(HEAD, z)
    behind = jnp.where(z > PAIR, z - 1 - HUB_LAST, z - 1 - head)
    head_decay = jnp.exp(
        -float(tokens) * jnp.maximum(behind, 0).astype(F32) * dec[...]
    )
    pair_decay = jnp.exp(
        -float(tokens) * jnp.maximum(z - 1 - PAIR, 0).astype(F32) * dec[...]
    )

    def receive_carry():
        carry[...] = jnp.zeros_like(carry)

        @pl.loop(jnp.where(z > PAIR, PAIR, head) + 1, z)
        def _(source):
            @pl.when(source != PAIR - 1)
            def _():
                arrived(source)

            carry[...] = carry[...] * decay_block + got[source].astype(F32)

        @pl.when(z > PAIR)
        def _():
            arrived(jnp.int32(PAIR))
            carry[...] += pair_decay * got[PAIR].astype(F32)

        @pl.when(z > 0)
        def _():
            arrived(head)
            carry[...] += head_decay * got[head].astype(F32)

    @pl.when(heads)
    def _():
        receive_carry()
        pre_msg[...] = (state[...] + decay_block * carry[...]).astype(BF16)
        for k in sorted({k for j in whole for k in whole[j]} - {PAIR}):

            @pl.when(z == k)
            def _():
                targets = [j for j in range(blocks) if k in whole[j]]
                send_whole(k, [j for j in targets if late.get(j) != k])
                if k in LATE and k != HUB:
                    pl.semaphore_wait(ready, len(LATE[k]))
                    send_whole(k, [j for j in targets if late.get(j) == k])

    def hub_step():
        @pl.when(z == HUB)
        def _():
            total = None
            for source in range(HUB_HEAD, HUB_LAST + 1):
                arrived(jnp.int32(source))
                block = got[source].astype(F32)
                total = block if total is None else total * decay_block + block
            hub_msg[...] = total.astype(BF16)
            pl.semaphore_wait(ready, len(HUB_TO))
            for j in reversed(HUB_TO):
                message(hub_msg, p_send, j).start()

    for half in range(2):
        lanes = pl.ds(half * (channels // 2), channels // 2)
        base = [gain[s, :, lanes] for s in range(modes)]
        for m in range(groups):
            kern[pl.ds(SUB * m, SUB), lanes] = sum(base[1:], base[0])
            if m + 1 < groups:
                base = [b * step8[s, :, lanes] for s, b in enumerate(base)]
    loads[5].wait()
    conv[...] = jnp.broadcast_to(skip[...], (tokens, channels)) * xpad[pl.ds(SUB, tokens), :]
    for m in range(groups):
        rows = tokens - SUB * m
        conv[pl.ds(SUB * m, rows), :] += sum(
            jnp.broadcast_to(kern[pl.ds(SUB * m + f, 1), :], (rows, channels))
            * xpad[pl.ds(SUB - f, rows), :]
            for f in range(SUB)
        )
    loads[4].wait()

    @pl.when(jnp.logical_not(heads))
    def _():
        receive_carry()

    for half in range(2):
        lanes = pl.ds(half * (channels // 2), channels // 2)
        base = [
            lead[s, :, lanes]
            * jnp.broadcast_to(carry[pl.ds(s, 1), lanes], (SUB, channels // 2))
            for s in range(modes)
        ]
        rows = []
        for m in range(groups):
            here = pl.ds(SUB * m, SUB)
            rows.append(
                q_in[here, lanes].astype(F32)
                * (conv[here, lanes] + sum(base[1:], base[0]))
            )
            if m + 1 < groups:
                base = [b * step8[s, :, lanes] for s, b in enumerate(base)]
        turned = [rows[SIDE * i + j] for j in range(SIDE) for i in range(SIDE)]
        for h, ordered in enumerate((rows, turned)):
            for m in range(0, groups, 2):
                gated[h, pl.ds(SUB * m, 2 * SUB), lanes] = jnp.concatenate(
                    ordered[m : m + 2], axis=0
                ).astype(BF16)

    loads[6].wait()
    place = (x, y)
    band = SIDE * SUB
    cut = band // LEVELS
    order = (2, 1, 3)
    steps = (1, SIDE - 1)
    pieces = [(r, h) for r in range(LEVELS) for h in range(2)]

    def at(h, shift):
        return (place[h] + shift) % SIDE

    def project(h):
        for side in range(2):
            value = jnp.dot(
                gated[h],
                weight[:, pl.ds(h * width + side * split, split)],
                preferred_element_type=F32,
            ).astype(BF16)
            for r in range(LEVELS):
                for i in range(SIDE):
                    start = i * band + r * cut
                    part[r, h, i, :, pl.ds(side * split, split)] = value[
                        start : start + cut
                    ]

    def first_copy(r, h, shift):
        return remote(
            part.at[r, h, at(h, shift)],
            part_in.at[r, h, shift - 1],
            r1_send.at[r, h, shift - 1],
            r1_recv.at[r, h, shift - 1],
            line(h, shift),
        )

    def opposite_copy(r, h, side):
        return remote(
            part.at[r, h, at(h, 2), :, pl.ds(side * split, split)],
            relay_in.at[r, h, side],
            a_send.at[r, h, side],
            a_recv.at[r, h, side],
            line(h, steps[side]),
        )

    def direct_copy(r, h, side):
        columns = pl.ds((1 - side) * split, split)
        return remote(
            part.at[r, h, at(h, steps[side]), :, columns],
            part_in.at[r, h, side, :, columns],
            r1_send.at[r, h, side],
            r1_recv.at[r, h, side],
            line(h, steps[side]),
        )

    def relay_copy(r, h, side):
        return remote(
            relay_out.at[r, h, side],
            part_in.at[r, h, side, :, pl.ds(side * split, split)],
            r1_send.at[r, h, 2 + side],
            r1_recv.at[r, h, 2 + side],
            line(h, steps[side]),
        )

    def second_copy(h, target, shift):
        return remote(
            half_sum.at[h, target],
            half_in.at[h, shift - 1],
            r2_send.at[h, shift - 1],
            r2_recv.at[h, shift - 1],
            line(1 - h, shift),
        )

    def second_phase(r, h, total):
        for i in range(LEVELS):
            rows = total[SUB * i : SUB * (i + 1)]
            target = LEVELS * r + i
            half_sum[h, target] = jnp.concatenate(
                [rows[:, :split], rows[:, split:]], axis=0
            ).astype(BF16)

            @pl.when(place[1 - h] != target)
            def _():
                second_copy(h, target, (target - place[1 - h] + SIDE) % SIDE).start()

    @pl.when(core == 0)
    def _():
        for h in range(2):
            project(h)
            first_copy(0, h, 2).start()
        for r in range(LEVELS):
            for h in range(2):
                if r > 0:
                    first_copy(r, h, 2).start()
            for h in range(2):
                for shift in (1, 3):
                    first_copy(r, h, shift).start()
        hub_step()
        for r, h in pieces:
            for shift in order:
                first_copy(r, h, shift).wait_send()
        pl.semaphore_signal(
            turn, inc=1, device_id={"dp": jnp.int32(1)}, device_id_type=MESH
        )
        for r, h in pieces:
            total = part[r, h, place[h]].astype(F32)
            for shift in order:
                first_copy(r, h, shift).wait_recv()
                total = total + part_in[r, h, shift - 1].astype(F32)
            second_phase(r, h, total)

    @pl.when(core == 1)
    def _():
        for h in range(2):
            project(h)
            for r in range(LEVELS):
                for side in range(2):
                    opposite_copy(r, h, side).start()
        for r, h in pieces:
            for side in range(2):
                direct_copy(r, h, side).start()
        hub_step()
        for r, h in pieces:
            for side in range(2):
                opposite_copy(r, h, side).wait_recv()
                mine = part[r, h, at(h, steps[side]), :, pl.ds(side * split, split)]
                relay_out[r, h, side] = (
                    mine.astype(F32) + relay_in[r, h, side].astype(F32)
                ).astype(BF16)
                relay_copy(r, h, side).start()
        pl.semaphore_wait(turn, 1)
        for r, h in pieces:
            for side in range(2):
                direct_copy(r, h, side).wait_recv()
                relay_copy(r, h, side).wait_recv()
            second_phase(
                r,
                h,
                part[r, h, place[h]].astype(F32)
                + part_in[r, h, 0].astype(F32)
                + part_in[r, h, 1].astype(F32),
            )

    @pl.when(core == 1)
    def _():
        for r, h in pieces:
            for side in range(2):
                opposite_copy(r, h, side).wait_send()
                direct_copy(r, h, side).wait_send()
                relay_copy(r, h, side).wait_send()

    for j in range(blocks):
        if plain[j]:

            @pl.when(among(plain[j]))
            def _():
                message(own_msg, e_send, j).wait_send()

        senders = whole[j] + ([HUB] if j in HUB_TO else [])
        if senders:

            @pl.when(among(senders))
            def _():
                message(pre_msg, p_send, j).wait_send()

    for h in range(2):
        for shift in order:
            second_copy(h, at(1 - h, shift), shift).wait_send()

    for h in range(2):
        total = half_sum[h, place[1 - h]].astype(F32)
        for shift in order:
            second_copy(h, place[1 - h], shift).wait_recv()
            total = total + half_in[h, shift - 1].astype(F32)
        for side in range(2):
            out_ref[:, pl.ds(h * width + side * split, split)] = total[
                SUB * side : SUB * (side + 1)
            ].astype(BF16)


def on_device(queries, keys, values, residues, decays, skip, out_weight):
    tokens, channels = keys.shape
    modes = residues.shape[1]
    features = out_weight.shape[1]
    blocks = len(HEAD)
    width = features // 2
    band = SIDE * SUB
    hbm = pl.BlockSpec(memory_space=pltpu.HBM)
    dma = pltpu.SemaphoreType.DMA
    return pl.pallas_call(
        operator_kernel,
        out_shape=pltpu.VMEM((SUB, features), BF16),
        in_specs=[hbm] * 7,
        out_specs=pl.BlockSpec(memory_space=pltpu.VMEM),
        scratch_shapes=[
            pltpu.VMEM((tokens, channels), BF16),
            pltpu.VMEM((tokens, channels), BF16),
            pltpu.VMEM((tokens, channels), BF16),
            pltpu.VMEM((modes, channels), F32),
            pltpu.VMEM((modes, channels), F32),
            pltpu.VMEM((1, channels), F32),
            pltpu.VMEM((channels, features), BF16),
            pltpu.VMEM((tokens + SUB, channels), F32),
            pltpu.VMEM((tokens, channels), F32),
            pltpu.VMEM((tokens, channels), F32),
            pltpu.VMEM((modes, SUB, channels), F32),
            pltpu.VMEM((modes, SUB, channels), F32),
            pltpu.VMEM((modes, SUB, channels), F32),
            pltpu.VMEM((modes, channels), F32),
            pltpu.VMEM((modes, channels), F32),
            pltpu.VMEM((modes, channels), BF16),
            pltpu.VMEM((modes, channels), BF16),
            pltpu.VMEM((modes, channels), BF16),
            pltpu.VMEM((blocks, modes, channels), BF16),
            pltpu.VMEM((2, tokens, channels), BF16),
            pltpu.VMEM((LEVELS, 2, SIDE, band // LEVELS, width), BF16),
            pltpu.VMEM((LEVELS, 2, SIDE - 1, band // LEVELS, width), BF16),
            pltpu.VMEM((LEVELS, 2, 2, band // LEVELS, width // 2), BF16),
            pltpu.VMEM((LEVELS, 2, 2, band // LEVELS, width // 2), BF16),
            pltpu.VMEM((2, SIDE, 2 * SUB, width // 2), BF16),
            pltpu.VMEM((2, SIDE - 1, 2 * SUB, width // 2), BF16),
            dma((7,)),
            dma((blocks,)),
            dma((blocks,)),
            dma((blocks,)),
            dma((LEVELS, 2, 2)),
            dma((LEVELS, 2, 2)),
            dma((LEVELS, 2, 4)),
            dma((LEVELS, 2, 4)),
            dma((2, SIDE - 1)),
            dma((2, SIDE - 1)),
            pltpu.SemaphoreType.REGULAR,
            pltpu.SemaphoreType.REGULAR,
        ],
        compiler_params=pltpu.CompilerParams(
            collective_id=0, has_side_effects=True, vmem_limit_bytes=60 << 20
        ),
    )(
        queries,
        keys,
        values,
        residues.T,
        decays.T,
        skip.reshape(1, channels),
        out_weight,
    )


def solution(mesh):
    placed = (
        P(("dp", "ctx"), "tp"),
        P(("dp", "ctx"), "tp"),
        P(("dp", "ctx"), "tp"),
        P("tp", None),
        P("tp", None),
        P("tp"),
        P("tp", None),
    )
    return jax.shard_map(
        on_device,
        mesh=mesh,
        in_specs=placed,
        out_specs=P(("dp", "ctx", "tp"), None),
        check_vma=False,
    )
```

```python
import functools

import jax
import jax.numpy as jnp
from jax import lax
from jax.experimental import pallas as pl
from jax.experimental.pallas import tpu as pltpu
from jax.sharding import PartitionSpec as P

MESH = pl.DeviceIdType.MESH
F32 = jnp.float32
BF16 = jnp.bfloat16

SIDE = 4
SUB = 8
HEAD = (0, 0, 1, 0, 3, 3, 3, 3, 6, 6, 6, 6, 0, 0, 0, 0)
HUB, HUB_HEAD, HUB_LAST, HUB_TO = 0, 3, 6, (12, 13, 14, 15)
PAIR = 8
PASS, PASS_TO = 7, (8, 9, 10, 11)
LATE = {HUB: HUB_TO, PASS: PASS_TO}
LEVELS = 2


def pick(table, index):
    value = jnp.int32(table[0])
    for position in range(1, len(table)):
        value = jnp.where(index == position, jnp.int32(table[position]), value)
    return value


def remote(src, dst, send_sem, recv_sem, device):
    return pltpu.make_async_remote_copy(
        src_ref=src,
        dst_ref=dst,
        send_sem=send_sem,
        recv_sem=recv_sem,
        device_id=device,
        device_id_type=MESH,
    )


def operator_kernel(
    q_hbm,
    k_hbm,
    v_hbm,
    res_hbm,
    dec_hbm,
    skip_hbm,
    w_hbm,
    out_ref,
    q_in,
    k_in,
    v_in,
    res,
    dec,
    skip,
    weight,
    xpad,
    kern,
    conv,
    gain,
    lead,
    step8,
    state,
    carry,
    own_msg,
    pre_msg,
    hub_msg,
    got,
    gated,
    part,
    part_in,
    relay_in,
    relay_out,
    half_sum,
    half_in,
    in_sem,
    e_send,
    p_send,
    c_recv,
    a_send,
    a_recv,
    r1_send,
    r1_recv,
    r2_send,
    r2_recv,
    ready,
    turn,
):
    blocks = len(HEAD)
    tokens, channels = k_in.shape
    groups = tokens // SUB
    modes = res.shape[0]
    width = part.shape[4]
    split = width // 2
    z = lax.axis_index("ctx")
    tp = lax.axis_index("tp")
    core = lax.axis_index("dp")
    x, y = tp // SIDE, tp % SIDE

    def line(axis, shift):
        if axis == 0:
            return {"tp": (x + shift) % SIDE * SIDE + y}
        return {"tp": x * SIDE + (y + shift) % SIDE}

    plain = {j: [] for j in range(blocks)}
    whole = {j: [] for j in range(blocks)}
    for j in range(1, blocks):
        start = HEAD[j] + 1 if j <= PAIR else PAIR + 1
        plain[j] += list(range(start, j))
        if j > PAIR:
            whole[j].append(PAIR)
        if j not in HUB_TO and j not in PASS_TO:
            whole[j].append(HEAD[j])
    plain[HUB] += list(range(HUB_HEAD + 1, HUB_LAST + 1))
    whole[HUB].append(HUB_HEAD)
    late = {j: k for k, group in LATE.items() for j in group}
    greeted = {j: plain[j] + whole[j] for j in range(blocks)}
    expected = pick(
        [
            sum(i in greeted[j] for j in range(blocks)) + (i in late)
            for i in range(blocks)
        ],
        z,
    )

    def among(members):
        members = sorted(members)
        spans = []
        for i in members:
            if spans and spans[-1][1] == i - 1:
                spans[-1][1] = i
            else:
                spans.append([i, i])
        return functools.reduce(
            jnp.logical_or,
            [
                z == low if low == high else jnp.logical_and(z >= low, z <= high)
                for low, high in spans
            ],
        )

    heads = among({k for j in range(blocks) for k in whole[j]} - {PAIR} | {PASS})
    barrier = pltpu.get_barrier_semaphore()

    for source in (*range(PAIR, blocks), *range(PAIR)):
        if any(source in greeted[j] for j in range(blocks)):

            @pl.when(among([j for j in range(blocks) if source in greeted[j]]))
            def _():
                pl.semaphore_signal(
                    barrier,
                    inc=1,
                    device_id={"ctx": jnp.int32(source)},
                    device_id_type=MESH,
                )

    for source, group in LATE.items():

        @pl.when(z == source)
        def _():
            for j in group:
                pl.semaphore_signal(
                    barrier,
                    inc=1,
                    device_id={"ctx": jnp.int32(j)},
                    device_id_type=MESH,
                )

    for shift in (2, 1, 3):
        for axis in (0, 1):
            pl.semaphore_signal(
                barrier, inc=1, device_id=line(axis, shift), device_id_type=MESH
            )

    @pl.when(core == 1)
    def _():
        pl.semaphore_signal(
            barrier, inc=1, device_id={"dp": jnp.int32(0)}, device_id_type=MESH
        )

    loads = [
        pltpu.make_async_copy(src, dst, in_sem.at[i])
        for i, (src, dst) in enumerate(
            (
                (k_hbm, k_in),
                (v_hbm, v_in),
                (dec_hbm, dec),
                (res_hbm, res),
                (q_hbm, q_in),
                (skip_hbm, skip),
                (w_hbm, weight),
            )
        )
    ]
    for load in loads:
        load.start()
    for load in loads[:4]:
        load.wait()

    xpad[pl.ds(0, SUB), :] = jnp.zeros((SUB, channels), F32)
    xpad[pl.ds(SUB, tokens), :] = k_in[...].astype(F32) * v_in[...].astype(F32)

    row = lax.broadcasted_iota(jnp.int32, (SUB, channels), 0).astype(F32)
    for s in range(modes):
        rate = jnp.broadcast_to(dec[pl.ds(s, 1), :], (SUB, channels))
        amp = jnp.broadcast_to(res[pl.ds(s, 1), :], (SUB, channels)) * jnp.sqrt(
            2.0 * rate
        )
        a8 = jnp.exp(-float(SUB) * rate)
        step8[s] = a8
        gain[s] = amp * jnp.exp(-rate * row)
        lead[s] = amp * jnp.exp(-rate * (row + 1.0))
        total = xpad[pl.ds(SUB, SUB), :]
        for m in range(1, groups):
            total = total * a8 + xpad[pl.ds(SUB * (m + 1), SUB), :]
        total = total * jnp.exp(rate * (row - float(SUB - 1)))
        state[pl.ds(s, 1), :] = jnp.sum(total, axis=0, keepdims=True)
    own_msg[...] = state[...].astype(BF16)
    decay_block = jnp.exp(-float(tokens) * dec[...])

    pl.semaphore_wait(barrier, 2 * (SIDE - 1) + expected + 1 - core)
    for source, group in LATE.items():

        @pl.when(among(group))
        def _():
            pl.semaphore_signal(
                ready,
                inc=1,
                device_id={"ctx": jnp.int32(source)},
                device_id_type=MESH,
            )

    def message(buffer, sems, j, slot=z):
        return remote(
            buffer, got.at[slot], sems.at[j], c_recv.at[slot], {"ctx": jnp.int32(j)}
        )

    def arrived(source):
        remote(
            own_msg, got.at[source], e_send.at[0], c_recv.at[source], {"ctx": z}
        ).wait_recv()

    def send_whole(k, targets):
        for j in reversed(targets):
            message(pre_msg, p_send, j).start()

    @pl.when(z == PAIR)
    def _():
        arrived(jnp.int32(PAIR - 1))
        pre_msg[...] = (
            state[...] + decay_block * got[PAIR - 1].astype(F32)
        ).astype(BF16)
        send_whole(PAIR, [j for j in range(blocks) if PAIR in whole[j]])

    for j in reversed(range(blocks)):
        if plain[j]:

            @pl.when(among(plain[j]))
            def _():
                message(own_msg, e_send, j).start()

    head = pick(HEAD, z)
    behind = jnp.where(z > PAIR, z - 1 - HUB_LAST, z - 1 - head)
    head_decay = jnp.exp(
        -float(tokens) * jnp.maximum(behind, 0).astype(F32) * dec[...]
    )
    pair_decay = jnp.exp(
        -float(tokens) * jnp.maximum(z - 1 - PAIR, 0).astype(F32) * dec[...]
    )

    def receive_carry():
        carry[...] = jnp.zeros_like(carry)

        @pl.loop(jnp.where(z > PAIR, PAIR, head) + 1, z)
        def _(source):
            @pl.when(source != PAIR - 1)
            def _():
                arrived(source)

            carry[...] = carry[...] * decay_block + got[source].astype(F32)

        @pl.when(z > PAIR)
        def _():
            arrived(jnp.int32(PAIR))
            carry[...] += pair_decay * got[PAIR].astype(F32)

        @pl.when(z > 0)
        def _():
            arrived(head)
            carry[...] += head_decay * got[head].astype(F32)

    @pl.when(heads)
    def _():
        receive_carry()
        pre_msg[...] = (state[...] + decay_block * carry[...]).astype(BF16)
        for k in sorted({k for j in whole for k in whole[j]} - {PAIR}):

            @pl.when(z == k)
            def _():
                send_whole(k, [j for j in range(blocks) if k in whole[j]])

        @pl.when(z == PASS)
        def _():
            pre_msg[...] = carry[...].astype(BF16)
            pl.semaphore_wait(ready, len(PASS_TO))
            for j in reversed(PASS_TO):
                message(pre_msg, p_send, j, jnp.int32(HUB_LAST)).start()

    def hub_step():
        @pl.when(z == HUB)
        def _():
            total = None
            for source in range(HUB_HEAD, HUB_LAST + 1):
                arrived(jnp.int32(source))
                block = got[source].astype(F32)
                total = block if total is None else total * decay_block + block
            hub_msg[...] = total.astype(BF16)
            pl.semaphore_wait(ready, len(HUB_TO))
            for j in reversed(HUB_TO):
                message(hub_msg, p_send, j).start()

    for half in range(2):
        lanes = pl.ds(half * (channels // 2), channels // 2)
        base = [gain[s, :, lanes] for s in range(modes)]
        for m in range(groups):
            kern[pl.ds(SUB * m, SUB), lanes] = sum(base[1:], base[0])
            if m + 1 < groups:
                base = [b * step8[s, :, lanes] for s, b in enumerate(base)]
    loads[5].wait()
    conv[...] = jnp.broadcast_to(skip[...], (tokens, channels)) * xpad[pl.ds(SUB, tokens), :]
    for m in range(groups):
        rows = tokens - SUB * m
        conv[pl.ds(SUB * m, rows), :] += sum(
            jnp.broadcast_to(kern[pl.ds(SUB * m + f, 1), :], (rows, channels))
            * xpad[pl.ds(SUB - f, rows), :]
            for f in range(SUB)
        )
    loads[4].wait()

    @pl.when(jnp.logical_not(heads))
    def _():
        receive_carry()

    for half in range(2):
        lanes = pl.ds(half * (channels // 2), channels // 2)
        base = [
            lead[s, :, lanes]
            * jnp.broadcast_to(carry[pl.ds(s, 1), lanes], (SUB, channels // 2))
            for s in range(modes)
        ]
        rows = []
        for m in range(groups):
            here = pl.ds(SUB * m, SUB)
            rows.append(
                q_in[here, lanes].astype(F32)
                * (conv[here, lanes] + sum(base[1:], base[0]))
            )
            if m + 1 < groups:
                base = [b * step8[s, :, lanes] for s, b in enumerate(base)]
        turned = [rows[SIDE * i + j] for j in range(SIDE) for i in range(SIDE)]
        for h, ordered in enumerate((rows, turned)):
            for m in range(0, groups, 2):
                gated[h, pl.ds(SUB * m, 2 * SUB), lanes] = jnp.concatenate(
                    ordered[m : m + 2], axis=0
                ).astype(BF16)

    loads[6].wait()
    place = (x, y)
    band = SIDE * SUB
    cut = band // LEVELS
    order = (2, 1, 3)
    steps = (1, SIDE - 1)
    pieces = [(r, h) for r in range(LEVELS) for h in range(2)]

    def at(h, shift):
        return (place[h] + shift) % SIDE

    def project(h):
        for side in range(2):
            value = jnp.dot(
                gated[h],
                weight[:, pl.ds(h * width + side * split, split)],
                preferred_element_type=F32,
            ).astype(BF16)
            for r in range(LEVELS):
                for i in range(SIDE):
                    start = i * band + r * cut
                    part[r, h, i, :, pl.ds(side * split, split)] = value[
                        start : start + cut
                    ]

    def first_copy(r, h, shift):
        return remote(
            part.at[r, h, at(h, shift)],
            part_in.at[r, h, shift - 1],
            r1_send.at[r, h, shift - 1],
            r1_recv.at[r, h, shift - 1],
            line(h, shift),
        )

    def opposite_copy(r, h, side):
        return remote(
            part.at[r, h, at(h, 2), :, pl.ds(side * split, split)],
            relay_in.at[r, h, side],
            a_send.at[r, h, side],
            a_recv.at[r, h, side],
            line(h, steps[side]),
        )

    def direct_copy(r, h, side):
        columns = pl.ds((1 - side) * split, split)
        return remote(
            part.at[r, h, at(h, steps[side]), :, columns],
            part_in.at[r, h, side, :, columns],
            r1_send.at[r, h, side],
            r1_recv.at[r, h, side],
            line(h, steps[side]),
        )

    def relay_copy(r, h, side):
        return remote(
            relay_out.at[r, h, side],
            part_in.at[r, h, side, :, pl.ds(side * split, split)],
            r1_send.at[r, h, 2 + side],
            r1_recv.at[r, h, 2 + side],
            line(h, steps[side]),
        )

    def second_copy(h, target, shift):
        return remote(
            half_sum.at[h, target],
            half_in.at[h, shift - 1],
            r2_send.at[h, shift - 1],
            r2_recv.at[h, shift - 1],
            line(1 - h, shift),
        )

    def second_phase(r, h, total):
        for i in range(LEVELS):
            rows = total[SUB * i : SUB * (i + 1)]
            target = LEVELS * r + i
            half_sum[h, target] = jnp.concatenate(
                [rows[:, :split], rows[:, split:]], axis=0
            ).astype(BF16)

            @pl.when(place[1 - h] != target)
            def _():
                second_copy(h, target, (target - place[1 - h] + SIDE) % SIDE).start()

    @pl.when(core == 0)
    def _():
        for h in range(2):
            project(h)
            first_copy(0, h, 2).start()
        for r in range(LEVELS):
            for h in range(2):
                if r > 0:
                    first_copy(r, h, 2).start()
            for h in range(2):
                for shift in (1, 3):
                    first_copy(r, h, shift).start()
        hub_step()
        for r, h in pieces:
            for shift in order:
                first_copy(r, h, shift).wait_send()
        pl.semaphore_signal(
            turn, inc=1, device_id={"dp": jnp.int32(1)}, device_id_type=MESH
        )
        for r, h in pieces:
            total = part[r, h, place[h]].astype(F32)
            for shift in order:
                first_copy(r, h, shift).wait_recv()
                total = total + part_in[r, h, shift - 1].astype(F32)
            second_phase(r, h, total)

    @pl.when(core == 1)
    def _():
        for h in range(2):
            project(h)
            for r in range(LEVELS):
                for side in range(2):
                    opposite_copy(r, h, side).start()
        for r, h in pieces:
            for side in range(2):
                direct_copy(r, h, side).start()
        hub_step()
        for r, h in pieces:
            for side in range(2):
                opposite_copy(r, h, side).wait_recv()
                mine = part[r, h, at(h, steps[side]), :, pl.ds(side * split, split)]
                relay_out[r, h, side] = (
                    mine.astype(F32) + relay_in[r, h, side].astype(F32)
                ).astype(BF16)
                relay_copy(r, h, side).start()
        pl.semaphore_wait(turn, 1)
        for r, h in pieces:
            for side in range(2):
                direct_copy(r, h, side).wait_recv()
                relay_copy(r, h, side).wait_recv()
            second_phase(
                r,
                h,
                part[r, h, place[h]].astype(F32)
                + part_in[r, h, 0].astype(F32)
                + part_in[r, h, 1].astype(F32),
            )

    @pl.when(core == 1)
    def _():
        for r, h in pieces:
            for side in range(2):
                opposite_copy(r, h, side).wait_send()
                direct_copy(r, h, side).wait_send()
                relay_copy(r, h, side).wait_send()

    for j in range(blocks):
        if plain[j]:

            @pl.when(among(plain[j]))
            def _():
                message(own_msg, e_send, j).wait_send()

        senders = whole[j] + [k for k in LATE if j in LATE[k]]
        if senders:

            @pl.when(among(senders))
            def _():
                message(pre_msg, p_send, j).wait_send()

    for h in range(2):
        for shift in order:
            second_copy(h, at(1 - h, shift), shift).wait_send()

    for h in range(2):
        total = half_sum[h, place[1 - h]].astype(F32)
        for shift in order:
            second_copy(h, place[1 - h], shift).wait_recv()
            total = total + half_in[h, shift - 1].astype(F32)
        for side in range(2):
            out_ref[:, pl.ds(h * width + side * split, split)] = total[
                SUB * side : SUB * (side + 1)
            ].astype(BF16)


def on_device(queries, keys, values, residues, decays, skip, out_weight):
    tokens, channels = keys.shape
    modes = residues.shape[1]
    features = out_weight.shape[1]
    blocks = len(HEAD)
    width = features // 2
    band = SIDE * SUB
    hbm = pl.BlockSpec(memory_space=pltpu.HBM)
    dma = pltpu.SemaphoreType.DMA
    return pl.pallas_call(
        operator_kernel,
        out_shape=pltpu.VMEM((SUB, features), BF16),
        in_specs=[hbm] * 7,
        out_specs=pl.BlockSpec(memory_space=pltpu.VMEM),
        scratch_shapes=[
            pltpu.VMEM((tokens, channels), BF16),
            pltpu.VMEM((tokens, channels), BF16),
            pltpu.VMEM((tokens, channels), BF16),
            pltpu.VMEM((modes, channels), F32),
            pltpu.VMEM((modes, channels), F32),
            pltpu.VMEM((1, channels), F32),
            pltpu.VMEM((channels, features), BF16),
            pltpu.VMEM((tokens + SUB, channels), F32),
            pltpu.VMEM((tokens, channels), F32),
            pltpu.VMEM((tokens, channels), F32),
            pltpu.VMEM((modes, SUB, channels), F32),
            pltpu.VMEM((modes, SUB, channels), F32),
            pltpu.VMEM((modes, SUB, channels), F32),
            pltpu.VMEM((modes, channels), F32),
            pltpu.VMEM((modes, channels), F32),
            pltpu.VMEM((modes, channels), BF16),
            pltpu.VMEM((modes, channels), BF16),
            pltpu.VMEM((modes, channels), BF16),
            pltpu.VMEM((blocks, modes, channels), BF16),
            pltpu.VMEM((2, tokens, channels), BF16),
            pltpu.VMEM((LEVELS, 2, SIDE, band // LEVELS, width), BF16),
            pltpu.VMEM((LEVELS, 2, SIDE - 1, band // LEVELS, width), BF16),
            pltpu.VMEM((LEVELS, 2, 2, band // LEVELS, width // 2), BF16),
            pltpu.VMEM((LEVELS, 2, 2, band // LEVELS, width // 2), BF16),
            pltpu.VMEM((2, SIDE, 2 * SUB, width // 2), BF16),
            pltpu.VMEM((2, SIDE - 1, 2 * SUB, width // 2), BF16),
            dma((7,)),
            dma((blocks,)),
            dma((blocks,)),
            dma((blocks,)),
            dma((LEVELS, 2, 2)),
            dma((LEVELS, 2, 2)),
            dma((LEVELS, 2, 4)),
            dma((LEVELS, 2, 4)),
            dma((2, SIDE - 1)),
            dma((2, SIDE - 1)),
            pltpu.SemaphoreType.REGULAR,
            pltpu.SemaphoreType.REGULAR,
        ],
        compiler_params=pltpu.CompilerParams(
            collective_id=0, has_side_effects=True, vmem_limit_bytes=60 << 20
        ),
    )(
        queries,
        keys,
        values,
        residues.T,
        decays.T,
        skip.reshape(1, channels),
        out_weight,
    )


def solution(mesh):
    placed = (
        P(("dp", "ctx"), "tp"),
        P(("dp", "ctx"), "tp"),
        P(("dp", "ctx"), "tp"),
        P("tp", None),
        P("tp", None),
        P("tp"),
        P("tp", None),
    )
    return jax.shard_map(
        on_device,
        mesh=mesh,
        in_specs=placed,
        out_specs=P(("dp", "ctx", "tp"), None),
        check_vma=False,
    )
```

```python
import functools

import jax
import jax.numpy as jnp
from jax import lax
from jax.experimental import pallas as pl
from jax.experimental.pallas import tpu as pltpu
from jax.sharding import PartitionSpec as P

MESH = pl.DeviceIdType.MESH
F32 = jnp.float32
BF16 = jnp.bfloat16

SIDE = 4
SUB = 8
HEAD = (0, 0, 1, 0, 3, 3, 3, 3, 6, 6, 6, 6, 0, 0, 0, 0)
HUB, HUB_HEAD, HUB_LAST, HUB_TO = 0, 3, 6, (12, 13, 14, 15)
PAIR = 8
PASS, PASS_TO = 7, (8, 9, 10, 11)
LATE = {HUB: HUB_TO, PASS: PASS_TO}
LEVELS = 2


def pick(table, index):
    value = jnp.int32(table[0])
    for position in range(1, len(table)):
        value = jnp.where(index == position, jnp.int32(table[position]), value)
    return value


def remote(src, dst, send_sem, recv_sem, device):
    return pltpu.make_async_remote_copy(
        src_ref=src,
        dst_ref=dst,
        send_sem=send_sem,
        recv_sem=recv_sem,
        device_id=device,
        device_id_type=MESH,
    )


def operator_kernel(
    q_hbm,
    k_hbm,
    v_hbm,
    res_hbm,
    dec_hbm,
    skip_hbm,
    w_hbm,
    out_ref,
    q_in,
    k_in,
    v_in,
    res,
    dec,
    skip,
    weight,
    xpad,
    kern,
    conv,
    gain,
    lead,
    step8,
    state,
    carry,
    own_msg,
    pre_msg,
    hub_msg,
    got,
    gated,
    part,
    part_in,
    relay_in,
    relay_out,
    half_sum,
    half_in,
    in_sem,
    e_send,
    p_send,
    c_recv,
    a_send,
    a_recv,
    r1_send,
    r1_recv,
    r2_send,
    r2_recv,
    ready,
    turn,
):
    blocks = len(HEAD)
    tokens, channels = k_in.shape
    groups = tokens // SUB
    modes = res.shape[0]
    width = part.shape[4]
    split = width // 2
    z = lax.axis_index("ctx")
    tp = lax.axis_index("tp")
    core = lax.axis_index("dp")
    x, y = tp // SIDE, tp % SIDE

    def line(axis, shift):
        if axis == 0:
            return {"tp": (x + shift) % SIDE * SIDE + y}
        return {"tp": x * SIDE + (y + shift) % SIDE}

    plain = {j: [] for j in range(blocks)}
    whole = {j: [] for j in range(blocks)}
    for j in range(1, blocks):
        start = HEAD[j] + 1 if j <= PAIR else PAIR + 1
        plain[j] += list(range(start, j))
        if j > PAIR:
            whole[j].append(PAIR)
        if j not in HUB_TO and j not in PASS_TO:
            whole[j].append(HEAD[j])
    plain[HUB] += list(range(HUB_HEAD + 1, HUB_LAST + 1))
    whole[HUB].append(HUB_HEAD)
    late = {j: k for k, group in LATE.items() for j in group}
    greeted = {j: plain[j] + whole[j] for j in range(blocks)}
    expected = pick(
        [
            sum(i in greeted[j] for j in range(blocks)) + (i in late)
            for i in range(blocks)
        ],
        z,
    )

    def among(members):
        members = sorted(members)
        spans = []
        for i in members:
            if spans and spans[-1][1] == i - 1:
                spans[-1][1] = i
            else:
                spans.append([i, i])
        return functools.reduce(
            jnp.logical_or,
            [
                z == low if low == high else jnp.logical_and(z >= low, z <= high)
                for low, high in spans
            ],
        )

    heads = among({k for j in range(blocks) for k in whole[j]} - {PAIR} | {PASS})
    barrier = pltpu.get_barrier_semaphore()

    for source in (*range(PAIR, blocks), *range(PAIR)):
        if any(source in greeted[j] for j in range(blocks)):

            @pl.when(among([j for j in range(blocks) if source in greeted[j]]))
            def _():
                pl.semaphore_signal(
                    barrier,
                    inc=1,
                    device_id={"ctx": jnp.int32(source)},
                    device_id_type=MESH,
                )

    for source, group in LATE.items():

        @pl.when(z == source)
        def _():
            for j in group:
                pl.semaphore_signal(
                    barrier,
                    inc=1,
                    device_id={"ctx": jnp.int32(j)},
                    device_id_type=MESH,
                )

    for shift in (2, 1, 3):
        for axis in (0, 1):
            pl.semaphore_signal(
                barrier, inc=1, device_id=line(axis, shift), device_id_type=MESH
            )

    @pl.when(core == 1)
    def _():
        pl.semaphore_signal(
            barrier, inc=1, device_id={"dp": jnp.int32(0)}, device_id_type=MESH
        )

    loads = [
        pltpu.make_async_copy(src, dst, in_sem.at[i])
        for i, (src, dst) in enumerate(
            (
                (k_hbm, k_in),
                (v_hbm, v_in),
                (dec_hbm, dec),
                (res_hbm, res),
                (q_hbm, q_in),
                (skip_hbm, skip),
                (w_hbm, weight),
            )
        )
    ]
    for load in loads:
        load.start()
    for load in loads[:4]:
        load.wait()

    xpad[pl.ds(0, SUB), :] = jnp.zeros((SUB, channels), F32)
    xpad[pl.ds(SUB, tokens), :] = k_in[...].astype(F32) * v_in[...].astype(F32)

    row = lax.broadcasted_iota(jnp.int32, (SUB, channels), 0).astype(F32)
    for s in range(modes):
        rate = jnp.broadcast_to(dec[pl.ds(s, 1), :], (SUB, channels))
        amp = jnp.broadcast_to(res[pl.ds(s, 1), :], (SUB, channels)) * jnp.sqrt(
            2.0 * rate
        )
        a8 = jnp.exp(-float(SUB) * rate)
        step8[s] = a8
        gain[s] = amp * jnp.exp(-rate * row)
        lead[s] = amp * jnp.exp(-rate * (row + 1.0))
        total = xpad[pl.ds(SUB, SUB), :]
        for m in range(1, groups):
            total = total * a8 + xpad[pl.ds(SUB * (m + 1), SUB), :]
        total = total * jnp.exp(rate * (row - float(SUB - 1)))
        state[pl.ds(s, 1), :] = jnp.sum(total, axis=0, keepdims=True)
    own_msg[...] = state[...].astype(BF16)
    decay_block = jnp.exp(-float(tokens) * dec[...])

    pl.semaphore_wait(barrier, 2 * (SIDE - 1) + expected + 1 - core)
    for source, group in LATE.items():

        @pl.when(among(group))
        def _():
            pl.semaphore_signal(
                ready,
                inc=1,
                device_id={"ctx": jnp.int32(source)},
                device_id_type=MESH,
            )

    def message(buffer, sems, j, slot=z):
        return remote(
            buffer, got.at[slot], sems.at[j], c_recv.at[slot], {"ctx": jnp.int32(j)}
        )

    def arrived(source):
        remote(
            own_msg, got.at[source], e_send.at[0], c_recv.at[source], {"ctx": z}
        ).wait_recv()

    def send_whole(k, targets):
        for j in reversed(targets):
            message(pre_msg, p_send, j).start()

    @pl.when(z == PAIR)
    def _():
        arrived(jnp.int32(PAIR - 1))
        pre_msg[...] = (
            state[...] + decay_block * got[PAIR - 1].astype(F32)
        ).astype(BF16)
        send_whole(PAIR, [j for j in range(blocks) if PAIR in whole[j]])

    for j in (0, *reversed(range(1, blocks))):
        if plain[j]:

            @pl.when(among(plain[j]))
            def _():
                message(own_msg, e_send, j).start()

    head = pick(HEAD, z)
    behind = jnp.where(z > PAIR, z - 1 - HUB_LAST, z - 1 - head)
    head_decay = jnp.exp(
        -float(tokens) * jnp.maximum(behind, 0).astype(F32) * dec[...]
    )
    pair_decay = jnp.exp(
        -float(tokens) * jnp.maximum(z - 1 - PAIR, 0).astype(F32) * dec[...]
    )

    def receive_carry():
        carry[...] = jnp.zeros_like(carry)

        @pl.loop(jnp.where(z > PAIR, PAIR, head) + 1, z)
        def _(source):
            @pl.when(source != PAIR - 1)
            def _():
                arrived(source)

            carry[...] = carry[...] * decay_block + got[source].astype(F32)

        @pl.when(jnp.logical_and(z > 0, z <= PAIR))
        def _():
            arrived(head)
            carry[...] += head_decay * got[head].astype(F32)

        @pl.when(z > PAIR)
        def _():
            arrived(jnp.int32(PAIR))
            known = carry[...] + pair_decay * got[PAIR].astype(F32)
            arrived(head)
            carry[...] = known + head_decay * got[head].astype(F32)

    @pl.when(heads)
    def _():
        receive_carry()
        pre_msg[...] = (state[...] + decay_block * carry[...]).astype(BF16)
        for k in sorted({k for j in whole for k in whole[j]} - {PAIR}):

            @pl.when(z == k)
            def _():
                send_whole(k, [j for j in range(blocks) if k in whole[j]])

        @pl.when(z == PASS)
        def _():
            pre_msg[...] = carry[...].astype(BF16)
            pl.semaphore_wait(ready, len(PASS_TO))
            for j in reversed(PASS_TO):
                message(pre_msg, p_send, j, jnp.int32(HUB_LAST)).start()

    def hub_step():
        @pl.when(z == HUB)
        def _():
            total = None
            for source in range(HUB_HEAD, HUB_LAST + 1):
                arrived(jnp.int32(source))
                block = got[source].astype(F32)
                total = block if total is None else total * decay_block + block
            hub_msg[...] = total.astype(BF16)
            pl.semaphore_wait(ready, len(HUB_TO))
            for j in HUB_TO:
                message(hub_msg, p_send, j).start()

    for half in range(2):
        lanes = pl.ds(half * (channels // 2), channels // 2)
        base = [gain[s, :, lanes] for s in range(modes)]
        for m in range(groups):
            kern[pl.ds(SUB * m, SUB), lanes] = sum(base[1:], base[0])
            if m + 1 < groups:
                base = [b * step8[s, :, lanes] for s, b in enumerate(base)]
    loads[5].wait()
    conv[...] = jnp.broadcast_to(skip[...], (tokens, channels)) * xpad[pl.ds(SUB, tokens), :]
    for m in range(groups):
        rows = tokens - SUB * m
        conv[pl.ds(SUB * m, rows), :] += sum(
            jnp.broadcast_to(kern[pl.ds(SUB * m + f, 1), :], (rows, channels))
            * xpad[pl.ds(SUB - f, rows), :]
            for f in range(SUB)
        )
    loads[4].wait()

    @pl.when(jnp.logical_not(heads))
    def _():
        receive_carry()

    for half in range(2):
        lanes = pl.ds(half * (channels // 2), channels // 2)
        base = [
            lead[s, :, lanes]
            * jnp.broadcast_to(carry[pl.ds(s, 1), lanes], (SUB, channels // 2))
            for s in range(modes)
        ]
        rows = []
        for m in range(groups):
            here = pl.ds(SUB * m, SUB)
            rows.append(
                q_in[here, lanes].astype(F32)
                * (conv[here, lanes] + sum(base[1:], base[0]))
            )
            if m + 1 < groups:
                base = [b * step8[s, :, lanes] for s, b in enumerate(base)]
        turned = [rows[SIDE * i + j] for j in range(SIDE) for i in range(SIDE)]
        for h, ordered in enumerate((rows, turned)):
            for m in range(0, groups, 2):
                gated[h, pl.ds(SUB * m, 2 * SUB), lanes] = jnp.concatenate(
                    ordered[m : m + 2], axis=0
                ).astype(BF16)

    loads[6].wait()
    place = (x, y)
    band = SIDE * SUB
    cut = band // LEVELS
    order = (2, 1, 3)
    steps = (1, SIDE - 1)
    pieces = [(r, h) for r in range(LEVELS) for h in range(2)]

    def at(h, shift):
        return (place[h] + shift) % SIDE

    def project(h):
        for side in range(2):
            value = jnp.dot(
                gated[h],
                weight[:, pl.ds(h * width + side * split, split)],
                preferred_element_type=F32,
            ).astype(BF16)
            for r in range(LEVELS):
                for i in range(SIDE):
                    start = i * band + r * cut
                    part[r, h, i, :, pl.ds(side * split, split)] = value[
                        start : start + cut
                    ]

    def first_copy(r, h, shift):
        return remote(
            part.at[r, h, at(h, shift)],
            part_in.at[r, h, shift - 1],
            r1_send.at[r, h, shift - 1],
            r1_recv.at[r, h, shift - 1],
            line(h, shift),
        )

    def opposite_copy(r, h, side):
        return remote(
            part.at[r, h, at(h, 2), :, pl.ds(side * split, split)],
            relay_in.at[r, h, side],
            a_send.at[r, h, side],
            a_recv.at[r, h, side],
            line(h, steps[side]),
        )

    def direct_copy(r, h, side):
        columns = pl.ds((1 - side) * split, split)
        return remote(
            part.at[r, h, at(h, steps[side]), :, columns],
            part_in.at[r, h, side, :, columns],
            r1_send.at[r, h, side],
            r1_recv.at[r, h, side],
            line(h, steps[side]),
        )

    def relay_copy(r, h, side):
        return remote(
            relay_out.at[r, h, side],
            part_in.at[r, h, side, :, pl.ds(side * split, split)],
            r1_send.at[r, h, 2 + side],
            r1_recv.at[r, h, 2 + side],
            line(h, steps[side]),
        )

    def second_copy(h, target, shift):
        return remote(
            half_sum.at[h, target],
            half_in.at[h, shift - 1],
            r2_send.at[h, shift - 1],
            r2_recv.at[h, shift - 1],
            line(1 - h, shift),
        )

    def second_phase(r, h, total):
        for i in range(LEVELS):
            rows = total[SUB * i : SUB * (i + 1)]
            target = LEVELS * r + i
            half_sum[h, target] = jnp.concatenate(
                [rows[:, :split], rows[:, split:]], axis=0
            ).astype(BF16)

            @pl.when(place[1 - h] != target)
            def _():
                second_copy(h, target, (target - place[1 - h] + SIDE) % SIDE).start()

    @pl.when(core == 0)
    def _():
        for h in range(2):
            project(h)
            first_copy(0, h, 2).start()
        for r in range(LEVELS):
            for h in range(2):
                if r > 0:
                    first_copy(r, h, 2).start()
            for h in range(2):
                for shift in (1, 3):
                    first_copy(r, h, shift).start()
        hub_step()
        for r, h in pieces:
            for shift in order:
                first_copy(r, h, shift).wait_send()
        pl.semaphore_signal(
            turn, inc=1, device_id={"dp": jnp.int32(1)}, device_id_type=MESH
        )
        for r, h in pieces:
            total = part[r, h, place[h]].astype(F32)
            for shift in order:
                first_copy(r, h, shift).wait_recv()
                total = total + part_in[r, h, shift - 1].astype(F32)
            second_phase(r, h, total)

    @pl.when(core == 1)
    def _():
        for h in range(2):
            project(h)
            for r in range(LEVELS):
                for side in range(2):
                    opposite_copy(r, h, side).start()
        for r, h in pieces:
            for side in range(2):
                direct_copy(r, h, side).start()
        hub_step()
        for r, h in pieces:
            for side in range(2):
                opposite_copy(r, h, side).wait_recv()
                mine = part[r, h, at(h, steps[side]), :, pl.ds(side * split, split)]
                relay_out[r, h, side] = (
                    mine.astype(F32) + relay_in[r, h, side].astype(F32)
                ).astype(BF16)
                relay_copy(r, h, side).start()
        pl.semaphore_wait(turn, 1)
        for r, h in pieces:
            for side in range(2):
                direct_copy(r, h, side).wait_recv()
                relay_copy(r, h, side).wait_recv()
            second_phase(
                r,
                h,
                part[r, h, place[h]].astype(F32)
                + part_in[r, h, 0].astype(F32)
                + part_in[r, h, 1].astype(F32),
            )

    @pl.when(core == 1)
    def _():
        for r, h in pieces:
            for side in range(2):
                opposite_copy(r, h, side).wait_send()
                direct_copy(r, h, side).wait_send()
                relay_copy(r, h, side).wait_send()

    for j in range(blocks):
        if plain[j]:

            @pl.when(among(plain[j]))
            def _():
                message(own_msg, e_send, j).wait_send()

        senders = whole[j] + [k for k in LATE if j in LATE[k]]
        if senders:

            @pl.when(among(senders))
            def _():
                message(pre_msg, p_send, j).wait_send()

    for h in range(2):
        for shift in order:
            second_copy(h, at(1 - h, shift), shift).wait_send()

    for h in range(2):
        total = half_sum[h, place[1 - h]].astype(F32)
        for shift in order:
            second_copy(h, place[1 - h], shift).wait_recv()
            total = total + half_in[h, shift - 1].astype(F32)
        for side in range(2):
            out_ref[:, pl.ds(h * width + side * split, split)] = total[
                SUB * side : SUB * (side + 1)
            ].astype(BF16)


def on_device(queries, keys, values, residues, decays, skip, out_weight):
    tokens, channels = keys.shape
    modes = residues.shape[1]
    features = out_weight.shape[1]
    blocks = len(HEAD)
    width = features // 2
    band = SIDE * SUB
    hbm = pl.BlockSpec(memory_space=pltpu.HBM)
    dma = pltpu.SemaphoreType.DMA
    return pl.pallas_call(
        operator_kernel,
        out_shape=pltpu.VMEM((SUB, features), BF16),
        in_specs=[hbm] * 7,
        out_specs=pl.BlockSpec(memory_space=pltpu.VMEM),
        scratch_shapes=[
            pltpu.VMEM((tokens, channels), BF16),
            pltpu.VMEM((tokens, channels), BF16),
            pltpu.VMEM((tokens, channels), BF16),
            pltpu.VMEM((modes, channels), F32),
            pltpu.VMEM((modes, channels), F32),
            pltpu.VMEM((1, channels), F32),
            pltpu.VMEM((channels, features), BF16),
            pltpu.VMEM((tokens + SUB, channels), F32),
            pltpu.VMEM((tokens, channels), F32),
            pltpu.VMEM((tokens, channels), F32),
            pltpu.VMEM((modes, SUB, channels), F32),
            pltpu.VMEM((modes, SUB, channels), F32),
            pltpu.VMEM((modes, SUB, channels), F32),
            pltpu.VMEM((modes, channels), F32),
            pltpu.VMEM((modes, channels), F32),
            pltpu.VMEM((modes, channels), BF16),
            pltpu.VMEM((modes, channels), BF16),
            pltpu.VMEM((modes, channels), BF16),
            pltpu.VMEM((blocks, modes, channels), BF16),
            pltpu.VMEM((2, tokens, channels), BF16),
            pltpu.VMEM((LEVELS, 2, SIDE, band // LEVELS, width), BF16),
            pltpu.VMEM((LEVELS, 2, SIDE - 1, band // LEVELS, width), BF16),
            pltpu.VMEM((LEVELS, 2, 2, band // LEVELS, width // 2), BF16),
            pltpu.VMEM((LEVELS, 2, 2, band // LEVELS, width // 2), BF16),
            pltpu.VMEM((2, SIDE, 2 * SUB, width // 2), BF16),
            pltpu.VMEM((2, SIDE - 1, 2 * SUB, width // 2), BF16),
            dma((7,)),
            dma((blocks,)),
            dma((blocks,)),
            dma((blocks,)),
            dma((LEVELS, 2, 2)),
            dma((LEVELS, 2, 2)),
            dma((LEVELS, 2, 4)),
            dma((LEVELS, 2, 4)),
            dma((2, SIDE - 1)),
            dma((2, SIDE - 1)),
            pltpu.SemaphoreType.REGULAR,
            pltpu.SemaphoreType.REGULAR,
        ],
        compiler_params=pltpu.CompilerParams(
            collective_id=0, has_side_effects=True, vmem_limit_bytes=60 << 20
        ),
    )(
        queries,
        keys,
        values,
        residues.T,
        decays.T,
        skip.reshape(1, channels),
        out_weight,
    )


def solution(mesh):
    placed = (
        P(("dp", "ctx"), "tp"),
        P(("dp", "ctx"), "tp"),
        P(("dp", "ctx"), "tp"),
        P("tp", None),
        P("tp", None),
        P("tp"),
        P("tp", None),
    )
    return jax.shard_map(
        on_device,
        mesh=mesh,
        in_specs=placed,
        out_specs=P(("dp", "ctx", "tp"), None),
        check_vma=False,
    )
```

```python
import functools

import jax
import jax.numpy as jnp
from jax import lax
from jax.experimental import pallas as pl
from jax.experimental.pallas import tpu as pltpu
from jax.sharding import PartitionSpec as P

MESH = pl.DeviceIdType.MESH
F32 = jnp.float32
BF16 = jnp.bfloat16

SIDE = 4
SUB = 8
HEAD = (0, 0, 1, 0, 3, 3, 3, 3, 6, 6, 6, 6, 0, 0, 0, 0)
HUB, HUB_HEAD, HUB_LAST, HUB_TO = 0, 3, 6, (12, 13, 14, 15)
PAIR = 8
PASS, PASS_TO = 7, (8, 9, 10, 11)
LATE = {HUB: HUB_TO, PASS: PASS_TO}
LEVELS = 2


def pick(table, index):
    value = jnp.int32(table[0])
    for position in range(1, len(table)):
        value = jnp.where(index == position, jnp.int32(table[position]), value)
    return value


def remote(src, dst, send_sem, recv_sem, device):
    return pltpu.make_async_remote_copy(
        src_ref=src,
        dst_ref=dst,
        send_sem=send_sem,
        recv_sem=recv_sem,
        device_id=device,
        device_id_type=MESH,
    )


def operator_kernel(
    q_hbm,
    k_hbm,
    v_hbm,
    res_hbm,
    dec_hbm,
    skip_hbm,
    w_hbm,
    out_ref,
    q_in,
    k_in,
    v_in,
    res,
    dec,
    skip,
    weight,
    xpad,
    kern,
    conv,
    gain,
    lead,
    step8,
    state,
    carry,
    own_msg,
    pre_msg,
    hub_msg,
    got,
    gated,
    part,
    part_in,
    relay_in,
    relay_out,
    half_sum,
    half_in,
    in_sem,
    e_send,
    p_send,
    c_recv,
    a_send,
    a_recv,
    r1_send,
    r1_recv,
    r2_send,
    r2_recv,
    ready,
    turn,
):
    blocks = len(HEAD)
    tokens, channels = k_in.shape
    groups = tokens // SUB
    modes = res.shape[0]
    width = part.shape[4]
    split = width // 2
    z = lax.axis_index("ctx")
    tp = lax.axis_index("tp")
    core = lax.axis_index("dp")
    x, y = tp // SIDE, tp % SIDE

    def line(axis, shift):
        if axis == 0:
            return {"tp": (x + shift) % SIDE * SIDE + y}
        return {"tp": x * SIDE + (y + shift) % SIDE}

    plain = {j: [] for j in range(blocks)}
    whole = {j: [] for j in range(blocks)}
    for j in range(1, blocks):
        start = HEAD[j] + 1 if j <= PAIR else PAIR + 1
        plain[j] += list(range(start, j))
        if j > PAIR:
            whole[j].append(PAIR)
        if j not in HUB_TO and j not in PASS_TO:
            whole[j].append(HEAD[j])
    plain[HUB] += list(range(HUB_HEAD + 1, HUB_LAST + 1))
    whole[HUB].append(HUB_HEAD)
    late = {j: k for k, group in LATE.items() for j in group}
    greeted = {j: plain[j] + whole[j] for j in range(blocks)}
    expected = pick(
        [
            sum(i in greeted[j] for j in range(blocks)) + (i in late)
            for i in range(blocks)
        ],
        z,
    )

    def among(members):
        members = sorted(members)
        spans = []
        for i in members:
            if spans and spans[-1][1] == i - 1:
                spans[-1][1] = i
            else:
                spans.append([i, i])
        return functools.reduce(
            jnp.logical_or,
            [
                z == low if low == high else jnp.logical_and(z >= low, z <= high)
                for low, high in spans
            ],
        )

    heads = among({k for j in range(blocks) for k in whole[j]} - {PAIR} | {PASS})
    barrier = pltpu.get_barrier_semaphore()

    for source in (*range(PAIR, blocks), *range(PAIR)):
        if any(source in greeted[j] for j in range(blocks)):

            @pl.when(among([j for j in range(blocks) if source in greeted[j]]))
            def _():
                pl.semaphore_signal(
                    barrier,
                    inc=1,
                    device_id={"ctx": jnp.int32(source)},
                    device_id_type=MESH,
                )

    for source, group in LATE.items():

        @pl.when(z == source)
        def _():
            for j in group:
                pl.semaphore_signal(
                    barrier,
                    inc=1,
                    device_id={"ctx": jnp.int32(j)},
                    device_id_type=MESH,
                )

    for shift in (2, 1, 3):
        for axis in (0, 1):
            pl.semaphore_signal(
                barrier, inc=1, device_id=line(axis, shift), device_id_type=MESH
            )

    @pl.when(core == 1)
    def _():
        pl.semaphore_signal(
            barrier, inc=1, device_id={"dp": jnp.int32(0)}, device_id_type=MESH
        )

    loads = [
        pltpu.make_async_copy(src, dst, in_sem.at[i])
        for i, (src, dst) in enumerate(
            (
                (k_hbm, k_in),
                (v_hbm, v_in),
                (dec_hbm, dec),
                (res_hbm, res),
                (q_hbm, q_in),
                (skip_hbm, skip),
                (w_hbm, weight),
            )
        )
    ]
    for load in loads:
        load.start()
    for load in loads[:4]:
        load.wait()

    xpad[pl.ds(0, SUB), :] = jnp.zeros((SUB, channels), F32)
    xpad[pl.ds(SUB, tokens), :] = k_in[...].astype(F32) * v_in[...].astype(F32)

    row = lax.broadcasted_iota(jnp.int32, (SUB, channels), 0).astype(F32)
    for s in range(modes):
        rate = jnp.broadcast_to(dec[pl.ds(s, 1), :], (SUB, channels))
        amp = jnp.broadcast_to(res[pl.ds(s, 1), :], (SUB, channels)) * jnp.sqrt(
            2.0 * rate
        )
        a8 = jnp.exp(-float(SUB) * rate)
        step8[s] = a8
        gain[s] = amp * jnp.exp(-rate * row)
        lead[s] = amp * jnp.exp(-rate * (row + 1.0))
        total = xpad[pl.ds(SUB, SUB), :]
        for m in range(1, groups):
            total = total * a8 + xpad[pl.ds(SUB * (m + 1), SUB), :]
        total = total * jnp.exp(rate * (row - float(SUB - 1)))
        state[pl.ds(s, 1), :] = jnp.sum(total, axis=0, keepdims=True)
    own_msg[...] = state[...].astype(BF16)
    decay_block = jnp.exp(-float(tokens) * dec[...])

    def message(buffer, sems, j, slot=z):
        return remote(
            buffer, got.at[slot], sems.at[j], c_recv.at[slot], {"ctx": jnp.int32(j)}
        )

    def arrived(source):
        remote(
            own_msg, got.at[source], e_send.at[0], c_recv.at[source], {"ctx": z}
        ).wait_recv()

    def send_whole(k, targets):
        for j in reversed(targets):
            message(pre_msg, p_send, j).start()

    @pl.when(z == PAIR)
    def _():
        arrived(jnp.int32(PAIR - 1))
        pre_msg[...] = (
            state[...] + decay_block * got[PAIR - 1].astype(F32)
        ).astype(BF16)

    pl.semaphore_wait(barrier, 2 * (SIDE - 1) + expected + 1 - core)
    for source, group in LATE.items():

        @pl.when(among(group))
        def _():
            pl.semaphore_signal(
                ready,
                inc=1,
                device_id={"ctx": jnp.int32(source)},
                device_id_type=MESH,
            )

    @pl.when(z == PAIR)
    def _():
        send_whole(PAIR, [j for j in range(blocks) if PAIR in whole[j]])

    for j in (0, *reversed(range(1, blocks))):
        if plain[j]:

            @pl.when(among(plain[j]))
            def _():
                message(own_msg, e_send, j).start()

    head = pick(HEAD, z)
    behind = jnp.where(z > PAIR, z - 1 - HUB_LAST, z - 1 - head)
    head_decay = jnp.exp(
        -float(tokens) * jnp.maximum(behind, 0).astype(F32) * dec[...]
    )
    pair_decay = jnp.exp(
        -float(tokens) * jnp.maximum(z - 1 - PAIR, 0).astype(F32) * dec[...]
    )

    def receive_carry():
        carry[...] = jnp.zeros_like(carry)

        @pl.loop(jnp.where(z > PAIR, PAIR, head) + 1, z)
        def _(source):
            @pl.when(source != PAIR - 1)
            def _():
                arrived(source)

            carry[...] = carry[...] * decay_block + got[source].astype(F32)

        @pl.when(jnp.logical_and(z > 0, z <= PAIR))
        def _():
            arrived(head)
            carry[...] += head_decay * got[head].astype(F32)

        @pl.when(z > PAIR)
        def _():
            arrived(jnp.int32(PAIR))
            known = carry[...] + pair_decay * got[PAIR].astype(F32)
            arrived(head)
            carry[...] = known + head_decay * got[head].astype(F32)

    @pl.when(heads)
    def _():
        receive_carry()
        pre_msg[...] = (state[...] + decay_block * carry[...]).astype(BF16)
        for k in sorted({k for j in whole for k in whole[j]} - {PAIR}):

            @pl.when(z == k)
            def _():
                send_whole(k, [j for j in range(blocks) if k in whole[j]])

        @pl.when(z == PASS)
        def _():
            pre_msg[...] = carry[...].astype(BF16)
            pl.semaphore_wait(ready, len(PASS_TO))
            for j in reversed(PASS_TO):
                message(pre_msg, p_send, j, jnp.int32(HUB_LAST)).start()

    def hub_step():
        @pl.when(z == HUB)
        def _():
            total = None
            for source in range(HUB_HEAD, HUB_LAST + 1):
                arrived(jnp.int32(source))
                block = got[source].astype(F32)
                total = block if total is None else total * decay_block + block
            hub_msg[...] = total.astype(BF16)
            pl.semaphore_wait(ready, len(HUB_TO))
            for j in HUB_TO:
                message(hub_msg, p_send, j).start()

    for half in range(2):
        lanes = pl.ds(half * (channels // 2), channels // 2)
        base = [gain[s, :, lanes] for s in range(modes)]
        for m in range(groups):
            kern[pl.ds(SUB * m, SUB), lanes] = sum(base[1:], base[0])
            if m + 1 < groups:
                base = [b * step8[s, :, lanes] for s, b in enumerate(base)]
    loads[5].wait()
    conv[...] = jnp.broadcast_to(skip[...], (tokens, channels)) * xpad[pl.ds(SUB, tokens), :]
    for m in range(groups):
        rows = tokens - SUB * m
        conv[pl.ds(SUB * m, rows), :] += sum(
            jnp.broadcast_to(kern[pl.ds(SUB * m + f, 1), :], (rows, channels))
            * xpad[pl.ds(SUB - f, rows), :]
            for f in range(SUB)
        )
    loads[4].wait()

    @pl.when(jnp.logical_not(heads))
    def _():
        receive_carry()

    for half in range(2):
        lanes = pl.ds(half * (channels // 2), channels // 2)
        base = [
            lead[s, :, lanes]
            * jnp.broadcast_to(carry[pl.ds(s, 1), lanes], (SUB, channels // 2))
            for s in range(modes)
        ]
        rows = []
        for m in range(groups):
            here = pl.ds(SUB * m, SUB)
            rows.append(
                q_in[here, lanes].astype(F32)
                * (conv[here, lanes] + sum(base[1:], base[0]))
            )
            if m + 1 < groups:
                base = [b * step8[s, :, lanes] for s, b in enumerate(base)]
        turned = [rows[SIDE * i + j] for j in range(SIDE) for i in range(SIDE)]
        for h, ordered in enumerate((rows, turned)):
            for m in range(0, groups, 2):
                gated[h, pl.ds(SUB * m, 2 * SUB), lanes] = jnp.concatenate(
                    ordered[m : m + 2], axis=0
                ).astype(BF16)

    loads[6].wait()
    place = (x, y)
    band = SIDE * SUB
    cut = band // LEVELS
    order = (2, 1, 3)
    steps = (1, SIDE - 1)
    pieces = [(r, h) for r in range(LEVELS) for h in range(2)]

    def at(h, shift):
        return (place[h] + shift) % SIDE

    def project(h):
        for side in range(2):
            value = jnp.dot(
                gated[h],
                weight[:, pl.ds(h * width + side * split, split)],
                preferred_element_type=F32,
            ).astype(BF16)
            for r in range(LEVELS):
                for i in range(SIDE):
                    start = i * band + r * cut
                    part[r, h, i, :, pl.ds(side * split, split)] = value[
                        start : start + cut
                    ]

    def first_copy(r, h, shift):
        return remote(
            part.at[r, h, at(h, shift)],
            part_in.at[r, h, shift - 1],
            r1_send.at[r, h, shift - 1],
            r1_recv.at[r, h, shift - 1],
            line(h, shift),
        )

    def opposite_copy(r, h, side):
        return remote(
            part.at[r, h, at(h, 2), :, pl.ds(side * split, split)],
            relay_in.at[r, h, side],
            a_send.at[r, h, side],
            a_recv.at[r, h, side],
            line(h, steps[side]),
        )

    def direct_copy(r, h, side):
        columns = pl.ds((1 - side) * split, split)
        return remote(
            part.at[r, h, at(h, steps[side]), :, columns],
            part_in.at[r, h, side, :, columns],
            r1_send.at[r, h, side],
            r1_recv.at[r, h, side],
            line(h, steps[side]),
        )

    def relay_copy(r, h, side):
        return remote(
            relay_out.at[r, h, side],
            part_in.at[r, h, side, :, pl.ds(side * split, split)],
            r1_send.at[r, h, 2 + side],
            r1_recv.at[r, h, 2 + side],
            line(h, steps[side]),
        )

    def second_copy(h, target, shift):
        return remote(
            half_sum.at[h, target],
            half_in.at[h, shift - 1],
            r2_send.at[h, shift - 1],
            r2_recv.at[h, shift - 1],
            line(1 - h, shift),
        )

    def second_phase(r, h, total):
        for i in range(LEVELS):
            rows = total[SUB * i : SUB * (i + 1)]
            target = LEVELS * r + i
            half_sum[h, target] = jnp.concatenate(
                [rows[:, :split], rows[:, split:]], axis=0
            ).astype(BF16)

            @pl.when(place[1 - h] != target)
            def _():
                second_copy(h, target, (target - place[1 - h] + SIDE) % SIDE).start()

    @pl.when(core == 0)
    def _():
        for h in range(2):
            project(h)
            first_copy(0, h, 2).start()
        for r in range(LEVELS):
            for h in range(2):
                if r > 0:
                    first_copy(r, h, 2).start()
            for h in range(2):
                for shift in (1, 3):
                    first_copy(r, h, shift).start()
        hub_step()
        for r, h in pieces:
            for shift in order:
                first_copy(r, h, shift).wait_send()
        pl.semaphore_signal(
            turn, inc=1, device_id={"dp": jnp.int32(1)}, device_id_type=MESH
        )
        for r, h in pieces:
            total = part[r, h, place[h]].astype(F32)
            for shift in order:
                first_copy(r, h, shift).wait_recv()
                total = total + part_in[r, h, shift - 1].astype(F32)
            second_phase(r, h, total)

    @pl.when(core == 1)
    def _():
        for h in range(2):
            project(h)
            for r in range(LEVELS):
                for side in range(2):
                    opposite_copy(r, h, side).start()
        for r, h in pieces:
            for side in range(2):
                direct_copy(r, h, side).start()
        hub_step()
        for r, h in pieces:
            for side in range(2):
                opposite_copy(r, h, side).wait_recv()
                mine = part[r, h, at(h, steps[side]), :, pl.ds(side * split, split)]
                relay_out[r, h, side] = (
                    mine.astype(F32) + relay_in[r, h, side].astype(F32)
                ).astype(BF16)
                relay_copy(r, h, side).start()
        pl.semaphore_wait(turn, 1)
        for r, h in pieces:
            for side in range(2):
                direct_copy(r, h, side).wait_recv()
                relay_copy(r, h, side).wait_recv()
            second_phase(
                r,
                h,
                part[r, h, place[h]].astype(F32)
                + part_in[r, h, 0].astype(F32)
                + part_in[r, h, 1].astype(F32),
            )

    @pl.when(core == 1)
    def _():
        for r, h in pieces:
            for side in range(2):
                opposite_copy(r, h, side).wait_send()
                direct_copy(r, h, side).wait_send()
                relay_copy(r, h, side).wait_send()

    for j in range(blocks):
        if plain[j]:

            @pl.when(among(plain[j]))
            def _():
                message(own_msg, e_send, j).wait_send()

        senders = whole[j] + [k for k in LATE if j in LATE[k]]
        if senders:

            @pl.when(among(senders))
            def _():
                message(pre_msg, p_send, j).wait_send()

    for h in range(2):
        for shift in order:
            second_copy(h, at(1 - h, shift), shift).wait_send()

    for h in range(2):
        total = half_sum[h, place[1 - h]].astype(F32)
        for shift in order:
            second_copy(h, place[1 - h], shift).wait_recv()
            total = total + half_in[h, shift - 1].astype(F32)
        for side in range(2):
            out_ref[:, pl.ds(h * width + side * split, split)] = total[
                SUB * side : SUB * (side + 1)
            ].astype(BF16)


def on_device(queries, keys, values, residues, decays, skip, out_weight):
    tokens, channels = keys.shape
    modes = residues.shape[1]
    features = out_weight.shape[1]
    blocks = len(HEAD)
    width = features // 2
    band = SIDE * SUB
    hbm = pl.BlockSpec(memory_space=pltpu.HBM)
    dma = pltpu.SemaphoreType.DMA
    return pl.pallas_call(
        operator_kernel,
        out_shape=pltpu.VMEM((SUB, features), BF16),
        in_specs=[hbm] * 7,
        out_specs=pl.BlockSpec(memory_space=pltpu.VMEM),
        scratch_shapes=[
            pltpu.VMEM((tokens, channels), BF16),
            pltpu.VMEM((tokens, channels), BF16),
            pltpu.VMEM((tokens, channels), BF16),
            pltpu.VMEM((modes, channels), F32),
            pltpu.VMEM((modes, channels), F32),
            pltpu.VMEM((1, channels), F32),
            pltpu.VMEM((channels, features), BF16),
            pltpu.VMEM((tokens + SUB, channels), F32),
            pltpu.VMEM((tokens, channels), F32),
            pltpu.VMEM((tokens, channels), F32),
            pltpu.VMEM((modes, SUB, channels), F32),
            pltpu.VMEM((modes, SUB, channels), F32),
            pltpu.VMEM((modes, SUB, channels), F32),
            pltpu.VMEM((modes, channels), F32),
            pltpu.VMEM((modes, channels), F32),
            pltpu.VMEM((modes, channels), BF16),
            pltpu.VMEM((modes, channels), BF16),
            pltpu.VMEM((modes, channels), BF16),
            pltpu.VMEM((blocks, modes, channels), BF16),
            pltpu.VMEM((2, tokens, channels), BF16),
            pltpu.VMEM((LEVELS, 2, SIDE, band // LEVELS, width), BF16),
            pltpu.VMEM((LEVELS, 2, SIDE - 1, band // LEVELS, width), BF16),
            pltpu.VMEM((LEVELS, 2, 2, band // LEVELS, width // 2), BF16),
            pltpu.VMEM((LEVELS, 2, 2, band // LEVELS, width // 2), BF16),
            pltpu.VMEM((2, SIDE, 2 * SUB, width // 2), BF16),
            pltpu.VMEM((2, SIDE - 1, 2 * SUB, width // 2), BF16),
            dma((7,)),
            dma((blocks,)),
            dma((blocks,)),
            dma((blocks,)),
            dma((LEVELS, 2, 2)),
            dma((LEVELS, 2, 2)),
            dma((LEVELS, 2, 4)),
            dma((LEVELS, 2, 4)),
            dma((2, SIDE - 1)),
            dma((2, SIDE - 1)),
            pltpu.SemaphoreType.REGULAR,
            pltpu.SemaphoreType.REGULAR,
        ],
        compiler_params=pltpu.CompilerParams(
            collective_id=0, has_side_effects=True, vmem_limit_bytes=60 << 20
        ),
    )(
        queries,
        keys,
        values,
        residues.T,
        decays.T,
        skip.reshape(1, channels),
        out_weight,
    )


def solution(mesh):
    placed = (
        P(("dp", "ctx"), "tp"),
        P(("dp", "ctx"), "tp"),
        P(("dp", "ctx"), "tp"),
        P("tp", None),
        P("tp", None),
        P("tp"),
        P("tp", None),
    )
    return jax.shard_map(
        on_device,
        mesh=mesh,
        in_specs=placed,
        out_specs=P(("dp", "ctx", "tp"), None),
        check_vma=False,
    )
```
